256 devices in a mesh: ctx: 16 (over x_lo, z), head: 2 (over core), ep: 8 (over y, x_hi).
Axes of the slice: x: 4 (x_hi: 2, x_lo: 2; x = x_hi * 2 + x_lo), y: 4, z: 8, core: 2. Of those that a mesh axis runs over, the one named last changes fastest.
Arguments:
- q_latent: bfloat16 [8192, 16, 576], P('ctx', ('head', 'ep')), may hold values from -20 to 20
- kv_latent: bfloat16 [8192, 576], P('ctx'), may hold values from -20 to 20
- w_value: bfloat16 [16, 512, 128], P(('head', 'ep')), may hold values from -0.25 to 0.25
- w_out: bfloat16 [2048, 2048], P(('head', 'ep')), may hold values from -0.125 to 0.125
- resid: bfloat16 [8192, 2048], P(('ctx', 'head', 'ep')), may hold values from -40 to 40
- norm_gain: float32 [2048], replicated, may hold values from 0.1 to 1.9
- w_gate: bfloat16 [16, 2048, 1408], P('ctx', None, 'head'), may hold values from -0.125 to 0.125
- w_up: bfloat16 [16, 2048, 1408], P('ctx', None, 'head'), may hold values from -0.125 to 0.125
- w_down_t: bfloat16 [16, 2048, 1408], P('ctx', None, 'head'), may hold values from -0.15625 to 0.15625
- expert_ids: int32 [8192, 6], P(('ctx', 'head', 'ep')), may hold values from 0 to 15, all different within a row; in each aligned block of 32 rows (0 to 31, 32 to 63, ...) at most 15 rows name the same one
- route_scores: float32 [8192, 6], P(('ctx', 'head', 'ep')), may hold values from 0.1 to 1
Outputs:
- layer_out: bfloat16 [8192, 2048], P(('ctx', 'head', 'ep'))
The draws below stay inside these ranges and needn't reach their ends.
Inputs may be any that keep to these rules, and one draw needn't show every extreme that they name: `expert_ids`: each row names 6 different experts. In each aligned block of 32 rows (the rows of one device) no expert is named by more than 15 rows, and in some block an expert is named by exactly 15 rows.
All inputs are finite; a program needn't handle non-finite values.
Results may differ from the reference program's by a relative error of at most 0.007.
Values may be sent and summed in bfloat16 or wider, within the bound.
A program may use at most 128 MiB of HBM per device.

```python
import math
import jax
import jax.numpy as jnp
import numpy as np
from jax import lax

D = 2048
HEADS = 16
LAT = 512
ROPE = 64
NOPE = 128
VDIM = 128
FF = 1408
TOPK = 6
L = 8192
EXPERTS = 16
ROWS = 32
CAP = 15


def attention_pair(key):
    base_key = jax.random.fold_in(key, 7103)
    width_all = LAT + ROPE
    latents = jax.random.truncated_normal(jax.random.fold_in(base_key, 1), -4.0, 4.0, (L, width_all), jnp.float32)
    queries = jax.random.truncated_normal(jax.random.fold_in(base_key, 2), -4.0, 4.0, (L, HEADS, width_all), jnp.float32)
    return (jnp.clip(queries, -20.0, 20.0), jnp.clip(latents, -20.0, 20.0))


def draw_q_latent(key, part):
    return attention_pair(key)[0].astype(jnp.bfloat16)


def draw_kv_latent(key, part):
    return attention_pair(key)[1].astype(jnp.bfloat16)


def draw_resid(key, part):
    base_key = jax.random.fold_in(key, 9241)
    row_scale = jnp.exp(jax.random.uniform(jax.random.fold_in(base_key, 1), (L, 1), jnp.float32, minval=math.log(0.3), maxval=math.log(3.0)))
    column_scale = jnp.exp(jax.random.uniform(jax.random.fold_in(base_key, 2), (1, D), jnp.float32, minval=math.log(0.3), maxval=math.log(3.0)))
    values = jax.random.truncated_normal(jax.random.fold_in(base_key, 4), -4.0, 4.0, (L, D), jnp.float32)
    return (values * row_scale * column_scale).astype(jnp.bfloat16)


def level_of(stream_key, shape, split, low, top_value):
    loudness, own = 1.0, jax.random.fold_in(stream_key, 6)
    for axis_at, blocks in split:
        heights = jnp.exp(jax.random.uniform(jax.random.fold_in(own, axis_at), (blocks,), jnp.float32, low / len(split), top_value / len(split)))
        loudness = loudness * jnp.repeat(heights, shape[axis_at] // blocks).reshape([-1 if axis == axis_at else 1 for axis in range(len(shape))])
    return loudness


def assign_block(key, own, number, rows, number_of, top, reach, skew):
    order = jax.random.permutation(key, number_of)
    crowded, ordinary = load_shares(number_of, rows * top, reach, skew, True), load_shares(number_of, rows * top, reach, skew, False)
    places = jnp.arange(number_of)

    def named(lengths, rotation):
        used = int((lengths > 0).sum())
        fixed = max(1, used // 4)
        moved = fixed + (places - fixed + rotation * (used - fixed)) % max(1, number_of - fixed)
        return jnp.zeros((number_of,), jnp.int32).at[order[jnp.where(places < fixed, places, moved)]].set(jnp.asarray(lengths, jnp.int32))

    lengths = jnp.where(number % 4 == 0, named(crowded, number // 4), named(ordinary, number - number // 4 - 1))
    mixed = jax.random.permutation(jax.random.fold_in(own, 3), number_of)
    source_of, receiver = mixed[0:number_of // 2 * 2:2], mixed[1:number_of // 2 * 2:2]
    margin = jnp.minimum(lengths[source_of] - 1, reach - lengths[receiver]) // 2
    margin = jnp.where((source_of == order[0]) | (receiver == order[0]) | (lengths[receiver] == 0), 0, jnp.maximum(margin, 0))
    moved = jax.random.randint(jax.random.fold_in(own, 4), (number_of // 2,), 0, 1 << 20) % (margin + 1)
    lengths = lengths.at[source_of].add(-moved).at[receiver].add(moved)
    labels = jnp.searchsorted(jnp.cumsum(lengths), jnp.arange(rows * top), side="right").astype(jnp.int32)
    table = labels.reshape(top, rows).T
    table = table[jax.random.permutation(jax.random.fold_in(own, 1), rows)]
    rotation = jax.random.randint(jax.random.fold_in(own, 2), (rows, 1), 0, top)
    return jnp.take_along_axis(table, (jnp.arange(top)[None, :] + rotation) % top, axis=1)


def load_shares(amount, total, reach, lean, full):
    weights = [(1 << 20) // math.isqrt(standing ** lean) + 1 for standing in range(1, amount + 1)]
    largest = reach if full else min(reach, max(-(-total // amount), total * weights[0] // sum(weights)))
    least = 1 if total - largest >= amount - 1 else 0
    holding, spare = [largest] + [least] * (amount - 1), total - largest - least * (amount - 1)
    while spare > 0:
        candidates = [i for i in range(1, amount) if holding[i] < largest] or [i for i in range(1, amount) if holding[i] < reach]
        pool, remaining = sum([weights[i] for i in candidates]), spare
        for i in candidates:
            more = min(reach - holding[i], max(1, remaining * weights[i] // pool), spare)
            holding[i] = holding[i] + more
            spare = spare - more
    return np.array(holding)


def bell_draw(rng, shape, width, limit, cuts=(), kind=jnp.bfloat16):
    drawn = jax.random.normal(rng, shape, jnp.float32) * width
    if len(cuts) > 0:
        drawn = level_of(rng, shape, cuts, -0.22, 0.18) * drawn
    return jnp.clip(drawn, min=-limit, max=limit).astype(kind)


def setup_inputs(seed: int = 0) -> dict:
    seeds = jax.random.split(jax.random.key(seed), 12)
    q_latent = draw_q_latent(jax.random.fold_in(seeds[11], 71), 0)
    kv_latent = draw_kv_latent(jax.random.fold_in(seeds[11], 71), 0)
    w_value = bell_draw(seeds[2], (HEADS, LAT, VDIM), LAT ** -0.5, 0.25, ((0, 16),))
    w_out = bell_draw(seeds[3], (HEADS * VDIM, D), (HEADS * VDIM) ** -0.5, 0.125, ((0, 16),))
    resid = draw_resid(jax.random.fold_in(seeds[11], 71), 0)
    norm_gain = jnp.clip(1.0 + 0.18 * jax.random.normal(seeds[5], (D,), jnp.float32), 0.1, 1.9)
    w_gate = bell_draw(seeds[6], (EXPERTS, D, FF), D ** -0.5, 0.125, ((0, 16), (2, 2)))
    w_up = bell_draw(seeds[7], (EXPERTS, D, FF), D ** -0.5, 0.125, ((0, 16), (2, 2)))
    w_down_t = bell_draw(seeds[8], (EXPERTS, D, FF), FF ** -0.5, 0.15625, ((0, 16), (2, 2)))
    expert_ids_keys = jax.random.split(jax.random.fold_in(seeds[9], 1), L // ROWS)
    expert_ids_turns = jax.random.permutation(jax.random.fold_in(seeds[9], 3), L // ROWS)
    expert_ids = jax.vmap(lambda own, number: assign_block(jax.random.fold_in(seeds[9], 2), own, number, ROWS, EXPERTS, TOPK, CAP, 2))(expert_ids_keys, expert_ids_turns).reshape((L, TOPK))
    route_scores = jnp.clip(jnp.exp(math.log(1.0) - 2.3025851 * jax.random.uniform(seeds[10], (L, TOPK), jnp.float32) ** level_of(seeds[10], (L, TOPK), ((0, 256),), -0.2, 0.2)), 0.1, 1.0)
    return dict(q_latent=q_latent, kv_latent=kv_latent, w_value=w_value, w_out=w_out, resid=resid, norm_gain=norm_gain, w_gate=w_gate, w_up=w_up, w_down_t=w_down_t, expert_ids=expert_ids, route_scores=route_scores)


routed_factor = 2.446
norm_epsilon = 1e-06
masked_score = -1e+30

def attend_heads(q_latent, kv_latent, w_value, w_out):
    block_rows = 1024 if L % 1024 == 0 else L
    score_scale = (NOPE + ROPE) ** (-0.5)

    def one_head(inputs):
        head_queries, head_value = inputs
        pieces = []
        for block in range(L // block_rows):
            begin = block * block_rows
            finish = begin + block_rows
            latents = kv_latent[:finish]
            scores = jnp.dot(head_queries[begin:finish], latents.T, preferred_element_type=jnp.float32) * score_scale
            query_pos = begin + jnp.arange(block_rows, dtype=jnp.int32)
            key_pos = jnp.arange(finish, dtype=jnp.int32)
            visible = key_pos[None, :] <= query_pos[:, None]
            scores = jnp.where(visible, scores, masked_score)
            highest = lax.optimization_barrier(jnp.max(scores, axis=1, keepdims=True))
            exponent_terms = jnp.where(visible, jnp.exp(scores - highest), 0.0)
            denominator = lax.optimization_barrier(jnp.sum(exponent_terms, axis=1, keepdims=True))
            weighted = jnp.dot(exponent_terms.astype(jnp.bfloat16), latents[:, :LAT], preferred_element_type=jnp.float32)
            latent_out = (weighted / denominator).astype(jnp.bfloat16)
            pieces.append(jnp.dot(latent_out, head_value, preferred_element_type=jnp.float32).astype(jnp.bfloat16))
        return jnp.concatenate(pieces, axis=0)
    per_head = lax.map(one_head, (jnp.moveaxis(q_latent, 1, 0), w_value))
    flat_heads = jnp.moveaxis(per_head, 0, 1).reshape(L, HEADS * VDIM)
    return jnp.dot(flat_heads, w_out, preferred_element_type=jnp.float32)

def reference(q_latent, kv_latent, w_value, w_out, resid, norm_gain, w_gate, w_up, w_down_t, expert_ids, route_scores):
    attended = attend_heads(q_latent, kv_latent, w_value, w_out)
    after_attn = lax.optimization_barrier((resid.astype(jnp.float32) + attended).astype(jnp.bfloat16))
    widened = after_attn.astype(jnp.float32)
    mean_square = lax.optimization_barrier(jnp.mean(widened * widened, axis=1, keepdims=True))
    normed_flat = (widened * lax.rsqrt(mean_square + norm_epsilon) * norm_gain).astype(jnp.bfloat16)
    token_count = L
    blocks = token_count // ROWS
    per_block = ROWS * TOPK
    chosen = expert_ids.reshape(blocks, per_block)
    onehot = (chosen[:, :, None] == jnp.arange(EXPERTS, dtype=jnp.int32)[None, None, :]).astype(jnp.int32)
    ranking = lax.optimization_barrier(jnp.sum(onehot * (jnp.cumsum(onehot, axis=1) - 1), axis=2)).astype(jnp.int32)
    block_index = jnp.broadcast_to(jnp.arange(blocks, dtype=jnp.int32)[:, None], (blocks, per_block))
    entry_index = jnp.broadcast_to(jnp.arange(per_block, dtype=jnp.int32)[None, :], (blocks, per_block))
    owners = jnp.full((blocks, EXPERTS, CAP), -1, jnp.int32).at[block_index, chosen, ranking].set(entry_index)
    present = owners >= 0
    entries = jnp.where(present, owners, 0).astype(jnp.int32)
    block_column = jnp.arange(blocks, dtype=jnp.int32)[:, None, None]
    token_of = (block_column * ROWS + entries // TOPK).astype(jnp.int32)
    combine = route_scores / lax.optimization_barrier(jnp.sum(route_scores, axis=1, keepdims=True))
    combine_flat = combine.reshape(blocks * per_block)
    weight_of = jnp.where(present, combine_flat[block_column * per_block + entries], 0.0)
    token_major = jnp.transpose(token_of, (1, 0, 2)).reshape(EXPERTS, blocks * CAP)
    weight_major = jnp.transpose(weight_of, (1, 0, 2)).reshape(EXPERTS, blocks * CAP)

    def add_expert(accum, inputs):
        gate_weight, up_weight, down_weight, token_ids, token_weights = inputs
        rows_in = normed_flat[token_ids]
        gate = jnp.dot(rows_in, gate_weight, preferred_element_type=jnp.float32)
        upward = jnp.dot(rows_in, up_weight, preferred_element_type=jnp.float32)
        hidden = (jax.nn.silu(gate) * upward).astype(jnp.bfloat16)
        produced = jnp.dot(hidden, down_weight.T, preferred_element_type=jnp.float32).astype(jnp.bfloat16)
        accum = accum.at[token_ids].add(produced.astype(jnp.float32) * token_weights[:, None])
        return (accum, None)
    accum, unused = lax.scan(add_expert, jnp.zeros((token_count, D), jnp.float32), (w_gate, w_up, w_down_t, token_major, weight_major))
    return (widened + routed_factor * accum).astype(jnp.bfloat16)
```

```python
import jax
import jax.numpy as jnp
from jax import lax
from jax.experimental import pallas as pl
from jax.experimental.pallas import tpu as pltpu
from jax.sharding import PartitionSpec as P

MESH = pl.DeviceIdType.MESH
BF16, F32 = jnp.bfloat16, jnp.float32
NT = (((1,), (1,)), ((), ()))
NN = (((1,), (0,)), ((), ()))
ROPE = 64
NOPE = 128
TOPK = 6
LOG2E = 1.4426950408889634
EXP_SCALE = (NOPE + ROPE) ** (-0.5) * LOG2E
routed_factor = 2.446
norm_epsilon = 1e-06
masked_score = -1e30


def dot(a, b, dims=NN):
    return lax.dot_general(a, b, dims, preferred_element_type=F32)


def coords():
    ctx, core, ep = lax.axis_index("ctx"), lax.axis_index("head"), lax.axis_index("ep")
    x_lo, z, y, x_hi = ctx // 8, ctx % 8, ep // 2, ep % 2
    return x_hi * 2 + x_lo, y, z, core


def device(x, y, z, core):
    x, y, z = (x + 4) % 4, (y + 4) % 4, (z + 8) % 8
    return ((x % 2) * 8 + z, core, y * 2 + x // 2)


def greet(partners):
    barrier = pltpu.get_barrier_semaphore()
    for partner in partners:
        pl.semaphore_signal(barrier, inc=1, device_id=partner, device_id_type=MESH)
    pl.semaphore_wait(barrier, len(partners))


def remote(src, dst, send_sem, recv_sem, target):
    return pltpu.make_async_remote_copy(
        src_ref=src, dst_ref=dst, send_sem=send_sem, recv_sem=recv_sem,
        device_id=target, device_id_type=MESH,
    )


SLOT = {0: 0, 1: 1, 7: 2, 2: 3, 6: 4, 3: 5, 5: 6, 4: 7}


def attention_kernel(
    q_ref, kv_ref, wv_ref, wo_ref, out_ref, wo4_ref,
    keys, q_far, wv_far, high, denom, accum, back, back_lse, far_out, far_lse,
    z_send, z_recv, y_send, y_recv, s_send, s_recv, q_send, q_recv, w_send, w_recv, own_sem,
):
    x, y, z, core = coords()
    x_lo, x_hi, parity = x % 2, x // 2, y % 2
    tokens, latent = q_ref.shape[0], wv_ref.shape[0]
    half, quarter = tokens // 2, tokens // 4
    z_up, z_down = device(x, y, z + 1, core), device(x, y, z - 1, core)
    y_up, y_down = device(x, y + 1, z, core), device(x, y - 1, z, core)
    x_up, x_down = device(x + 1, y, z, core), device(x - 1, y, z, core)
    sibling = device(x, y, z, 1 - core)
    y_to = device(x, y + 1 - 2 * core, z, core)
    x_to = device(x - 1 + 2 * core, y, z, core)
    x_from = device(x + 1 - 2 * core, y, z, core)
    x_other = device(x - 1 + 2 * x_lo, y, z, core)

    row_mine = parity * half + core * quarter
    row_other = (1 - parity) * half + core * quarter
    row_sib_mine = parity * half + (1 - core) * quarter
    row_sib_other = (1 - parity) * half + (1 - core) * quarter

    def rows(k, start, size):
        return keys.at[pl.ds(pl.multiple_of(SLOT[k] * tokens + start, 16), size)]

    def z_copy(way, step):
        target = z_up if way == 0 else z_down
        k_dst = step if way == 0 else 8 - step
        k_src = step - 1 if way == 0 else (8 - (step - 1)) % 8
        start, size = row_mine, quarter
        if step == 4:
            size = quarter // 2
            start = row_mine + way * size
        if k_src == 0:
            src = kv_ref.at[pl.ds(pl.multiple_of(start, 16), size)]
        else:
            src = rows(k_src, start, size)
        return remote(src, rows(k_dst, start, size), z_send.at[way, step - 1], z_recv.at[way, step - 1], target)

    def y_copy(k, start):
        return remote(rows(k, start, quarter), rows(k, start, quarter), y_send.at[k - 1], y_recv.at[k - 1], y_to)

    def s_copy(k, which, start):
        return remote(rows(k, start, quarter), rows(k, start, quarter), s_send.at[which, k - 1], s_recv.at[which, k - 1], sibling)

    q_copy = remote(q_ref, q_far, q_send.at[0], q_recv.at[0], x_to)
    wv_copy = remote(wv_ref, wv_far, q_send.at[1], q_recv.at[1], x_to)
    back_copy = remote(back, far_out, q_send.at[2], q_recv.at[2], x_from)
    lse_copy = remote(back_lse, far_lse, q_send.at[3], q_recv.at[3], x_from)
    mine, partner = core * 2 + x_hi, core * 2 + 1 - x_hi
    wo_own = pltpu.make_async_copy(wo_ref, wo4_ref.at[mine], own_sem)
    wo_sib = remote(wo_ref, wo4_ref.at[mine], w_send.at[0], w_recv.at[0], sibling)
    wo_far = remote(wo_ref, wo4_ref.at[mine], w_send.at[1], w_recv.at[1], x_other)
    wo_fwd = remote(wo4_ref.at[partner], wo4_ref.at[partner], w_send.at[2], w_recv.at[2], sibling)

    greet([z_up, z_down, y_up, y_down, x_up, x_down, sibling])

    z_copy(0, 1).start()
    z_copy(1, 1).start()

    @pl.when(x_lo == 1)
    def _():
        q_copy.start()
        wv_copy.start()

    wo_own.start()
    wo_sib.start()
    wo_far.start()

    keys[0:tokens] = kv_ref[...]
    high[...] = jnp.full(high.shape, masked_score, F32)
    denom[...] = jnp.zeros(denom.shape, F32)
    accum[...] = jnp.zeros(accum.shape, F32)

    def tile(which, queries, slot, count, change=None):
        block = keys[slot * tokens:(slot + count) * tokens]
        chunks = [slice(0, half), slice(half, tokens)]
        scores = [dot(queries[rows_at], block, NT) for rows_at in chunks]
        for rows_at, score in zip(chunks, scores):
            if change is not None:
                score = change(score, rows_at.start)
            at = (which, rows_at, slice(None))
            old = high[at]
            new = jnp.maximum(old, jnp.max(score, axis=1, keepdims=True))
            keep = jnp.exp2((old - new) * EXP_SCALE)
            weight = jnp.exp2((score - new) * EXP_SCALE)
            denom[at] = denom[at] * keep + jnp.sum(weight, axis=1, keepdims=True)
            high[at] = new
            accum[at] = accum[at] * keep + dot(weight.astype(BF16), block[:, :latent])

    def diagonal(score, start):
        row = start + lax.broadcasted_iota(jnp.int32, score.shape, 0)
        column = lax.broadcasted_iota(jnp.int32, score.shape, 1)
        return jnp.where(column <= row, score, masked_score)

    def pair_mask(step):
        def change(score, start):
            column = lax.broadcasted_iota(jnp.int32, score.shape, 1)
            first = jnp.where(z >= step, 0, tokens)
            last = jnp.where(z + step >= 8, 2 * tokens, tokens)
            return jnp.where((column >= first) & (column < last), score, masked_score)
        return change

    def own_pair(step):
        both = (z >= step) & (z + step >= 8)
        some = (z >= step) | (z + step >= 8)

        @pl.when(both)
        def _():
            tile(0, q_ref, SLOT[step], 2)

        @pl.when(some & jnp.logical_not(both))
        def _():
            tile(0, q_ref, SLOT[step], 2, pair_mask(step))

    def far_tile(slot, count):
        @pl.when(x_lo == 0)
        def _():
            tile(1, q_far, slot, count)

    tile(0, q_ref, 0, 1, diagonal)

    def after_z(step):
        ks = [step, 8 - step] if step < 4 else [4]
        z_copy(0, step).wait_recv()
        z_copy(1, step).wait_recv()
        if step < 4:
            z_copy(0, step + 1).start()
            z_copy(1, step + 1).start()
        for k in ks:
            y_copy(k, row_mine).start()
            s_copy(k, 0, row_mine).start()

    def after_y(step):
        for k in ([step, 8 - step] if step < 4 else [4]):
            y_copy(k, row_other).wait_recv()
            s_copy(k, 1, row_other).start()

    def after_s(step):
        for k in ([step, 8 - step] if step < 4 else [4]):
            s_copy(k, 0, row_sib_mine).wait_recv()
            s_copy(k, 1, row_sib_other).wait_recv()

    after_z(1)
    after_y(1)

    @pl.when(x_lo == 0)
    def _():
        q_copy.wait_recv()
        wv_copy.wait_recv()

    far_tile(0, 1)
    after_z(2)
    after_s(1)
    own_pair(1)
    after_y(2)
    far_tile(1, 2)
    after_z(3)
    after_s(2)
    own_pair(2)
    after_y(3)
    far_tile(3, 2)
    after_z(4)
    after_s(3)
    own_pair(3)
    after_y(4)
    far_tile(5, 2)
    wo_far.wait_recv()
    wo_fwd.start()
    after_s(4)
    far_tile(7, 1)

    @pl.when(x_lo == 0)
    def _():
        latent_far = (accum[1] / denom[1]).astype(BF16)
        back[...] = dot(latent_far, wv_far[...]).astype(BF16)
        lse = high[1] * EXP_SCALE + jnp.log2(denom[1])
        back_lse[...] = jnp.broadcast_to(lse, (tokens, 128)).T[0:8]
        back_copy.start()
        lse_copy.start()

    @pl.when(z >= 4)
    def _():
        tile(0, q_ref, 7, 1)

    head_out = dot((accum[0] / denom[0]).astype(BF16), wv_ref[...])

    @pl.when(x_lo == 0)
    def _():
        out_ref[...] = head_out.astype(BF16)

    @pl.when(x_lo == 1)
    def _():
        lse = high[0] * EXP_SCALE + jnp.log2(denom[0])
        back_copy.wait_recv()
        lse_copy.wait_recv()
        other = jnp.broadcast_to(far_lse[0:1], (128, tokens)).T
        top = jnp.maximum(lse, other)
        near_part, far_part = jnp.exp2(lse - top), jnp.exp2(other - top)
        out_ref[...] = ((head_out * near_part + far_out[...].astype(F32) * far_part) / (near_part + far_part)).astype(BF16)

    wo_sib.wait_recv()
    wo_fwd.wait_recv()
    wo_own.wait()
    for copy in (wo_sib, wo_far, wo_fwd):
        copy.wait_send()
    for step in range(1, 5):
        z_copy(0, step).wait_send()
        z_copy(1, step).wait_send()
    for k in range(1, 8):
        y_copy(k, row_mine).wait_send()
        s_copy(k, 0, row_mine).wait_send()
        s_copy(k, 1, row_other).wait_send()

    @pl.when(x_lo == 1)
    def _():
        q_copy.wait_send()
        wv_copy.wait_send()

    @pl.when(x_lo == 0)
    def _():
        back_copy.wait_send()
        lse_copy.wait_send()


def attend(queries, kv, w_value, w_out):
    tokens, width = queries.shape
    latent, values = w_value.shape
    dma = pltpu.SemaphoreType.DMA
    vmem = pl.BlockSpec(memory_space=pltpu.VMEM)
    hbm = pl.BlockSpec(memory_space=pl.ANY)
    return pl.pallas_call(
        attention_kernel,
        out_shape=(
            jax.ShapeDtypeStruct((tokens, values), BF16),
            jax.ShapeDtypeStruct((4,) + w_out.shape, BF16),
        ),
        in_specs=[vmem, vmem, vmem, hbm],
        out_specs=(vmem, hbm),
        scratch_shapes=[
            pltpu.VMEM((8 * tokens, width), BF16),
            pltpu.VMEM((tokens, width), BF16),
            pltpu.VMEM((latent, values), BF16),
            pltpu.VMEM((2, tokens, 1), F32),
            pltpu.VMEM((2, tokens, 1), F32),
            pltpu.VMEM((2, tokens, latent), F32),
            pltpu.VMEM((tokens, values), BF16),
            pltpu.VMEM((8, tokens), F32),
            pltpu.VMEM((tokens, values), BF16),
            pltpu.VMEM((8, tokens), F32),
            dma((2, 4)), dma((2, 4)), dma((7,)), dma((7,)), dma((2, 7)), dma((2, 7)),
            dma((4,)), dma((4,)), dma((3,)), dma((3,)), dma,
        ],
        name="attention",
        compiler_params=pltpu.CompilerParams(collective_id=0, has_side_effects=True, vmem_limit_bytes=56 << 20),
    )(queries, kv, w_value, w_out)


def expert_half(inputs, gate_part, up_part, down_part):
    gate = jnp.dot(inputs, gate_part, preferred_element_type=jnp.float32)
    upward = jnp.dot(inputs, up_part, preferred_element_type=jnp.float32)
    hidden = (jax.nn.silu(gate) * upward).astype(jnp.bfloat16)
    return lax.dot_general(
        hidden, down_part, (((1,), (1,)), ((), ())), preferred_element_type=jnp.float32
    )


def make_projection(source, piece):
    return jnp.dot(source, piece, preferred_element_type=jnp.float32)


def per_device(
    q_latent,
    kv_latent,
    w_value,
    w_out,
    resid,
    norm_gain,
    w_gate,
    w_up,
    w_down_t,
    expert_ids,
    route_scores,
):
    tokens_here = q_latent.shape[0]
    heads_here = q_latent.shape[1]
    latent_width = w_value.shape[1]
    width = resid.shape[1]
    rows = resid.shape[0]
    head_out, _ = attend(q_latent.reshape(tokens_here, q_latent.shape[2]), kv_latent, w_value[0], w_out)
    head_out = head_out.reshape(tokens_here, 1, w_value.shape[2])
    grouped = lax.all_to_all(head_out, ("head", "ep"), split_axis=0, concat_axis=1, tiled=True)
    flat_heads = grouped.reshape(rows, grouped.shape[1] * grouped.shape[2])
    attended = make_projection(
        flat_heads, lax.all_gather(w_out, ("head", "ep"), axis=0, tiled=True)
    )
    after_attn = lax.optimization_barrier(
        (resid.astype(jnp.float32) + attended).astype(jnp.bfloat16)
    )
    widened = after_attn.astype(jnp.float32)
    mean_square = jnp.mean(widened * widened, axis=1, keepdims=True)
    normed = (widened * lax.rsqrt(mean_square + norm_epsilon) * norm_gain).astype(jnp.bfloat16)
    experts_here = lax.axis_size("ctx")
    capacity = 5 * rows * TOPK // (4 * experts_here)
    chosen = expert_ids.reshape(rows * TOPK)
    onehot = (chosen[:, None] == jnp.arange(experts_here, dtype=jnp.int32)[None, :]).astype(
        jnp.int32
    )
    ranking = jnp.sum(onehot * (jnp.cumsum(onehot, axis=0) - 1), axis=1)
    slot_ids = chosen * capacity + ranking
    slot_table = jnp.arange(experts_here * capacity, dtype=jnp.int32)
    placing = jnp.any(slot_ids.reshape(rows, TOPK)[None, :, :] == slot_table[:, None, None], axis=2)
    dispatch = jnp.dot(
        placing.astype(jnp.bfloat16), normed, preferred_element_type=jnp.float32
    ).astype(jnp.bfloat16)
    dispatch = dispatch.reshape(experts_here, capacity, width)
    arrived = lax.all_to_all(dispatch, "ctx", split_axis=0, concat_axis=0, tiled=True)
    pooled = lax.all_gather(arrived, "head", axis=0, tiled=True).reshape(-1, width)
    produced = lax.psum_scatter(
        expert_half(pooled, w_gate[0], w_up[0], w_down_t[0]).astype(jnp.bfloat16),
        "head",
        scatter_dimension=0,
        tiled=True,
    )
    outgoing = produced.reshape(experts_here, capacity, width)
    returned = lax.all_to_all(outgoing, "ctx", split_axis=0, concat_axis=0, tiled=True)
    picked = returned.reshape(experts_here * capacity, width)[slot_ids].reshape(rows, TOPK, width)
    combine = route_scores / jnp.sum(route_scores, axis=1, keepdims=True)
    combined = jnp.sum(picked.astype(jnp.float32) * combine[:, :, None], axis=1)
    return (widened + routed_factor * combined).astype(jnp.bfloat16)


def solution(mesh):
    placed = (
        P("ctx", ("head", "ep"), None),
        P("ctx", None),
        P(("head", "ep"), None, None),
        P(("head", "ep"), None),
        P(("ctx", "head", "ep"), None),
        P(),
        P("ctx", None, "head"),
        P("ctx", None, "head"),
        P("ctx", None, "head"),
        P(("ctx", "head", "ep"), None),
        P(("ctx", "head", "ep"), None),
    )
    return jax.shard_map(
        per_device,
        mesh=mesh,
        in_specs=placed,
        out_specs=P(("ctx", "head", "ep"), None),
        check_vma=False,
    )
```

```python
import jax
import jax.numpy as jnp
from jax import lax
from jax.experimental import pallas as pl
from jax.experimental.pallas import tpu as pltpu
from jax.sharding import PartitionSpec as P

MESH = pl.DeviceIdType.MESH
BF16, F32 = jnp.bfloat16, jnp.float32
NT = (((1,), (1,)), ((), ()))
NN = (((1,), (0,)), ((), ()))
ROPE = 64
NOPE = 128
TOPK = 6
LOG2E = 1.4426950408889634
EXP_SCALE = (NOPE + ROPE) ** (-0.5) * LOG2E
routed_factor = 2.446
norm_epsilon = 1e-06
masked_score = -1e30


def dot(a, b, dims=NN):
    return lax.dot_general(a, b, dims, preferred_element_type=F32)


def coords():
    ctx, core, ep = lax.axis_index("ctx"), lax.axis_index("head"), lax.axis_index("ep")
    x_lo, z, y, x_hi = ctx // 8, ctx % 8, ep // 2, ep % 2
    return x_hi * 2 + x_lo, y, z, core


def device(x, y, z, core):
    x, y, z = (x + 4) % 4, (y + 4) % 4, (z + 8) % 8
    return ((x % 2) * 8 + z, core, y * 2 + x // 2)


def greet(partners):
    barrier = pltpu.get_barrier_semaphore()
    for partner in partners:
        pl.semaphore_signal(barrier, inc=1, device_id=partner, device_id_type=MESH)
    pl.semaphore_wait(barrier, len(partners))


def remote(src, dst, send_sem, recv_sem, target):
    return pltpu.make_async_remote_copy(
        src_ref=src, dst_ref=dst, send_sem=send_sem, recv_sem=recv_sem,
        device_id=target, device_id_type=MESH,
    )


SLOT = {0: 0, 1: 1, 7: 2, 2: 3, 6: 4, 3: 5, 5: 6, 4: 7}


def attention_kernel(
    q_ref, kv_ref, wv_ref, wo_ref, out_ref, wo4_ref,
    keys, q_far, wv_far, high, denom, accum, back, back_lse, far_out, far_lse,
    z_send, z_recv, y_send, y_recv, s_send, s_recv, q_send, q_recv, w_send, w_recv, own_sem,
):
    x, y, z, core = coords()
    x_lo, x_hi, parity = x % 2, x // 2, y % 2
    tokens, latent = q_ref.shape[0], wv_ref.shape[0]
    half, quarter = tokens // 2, tokens // 4
    z_up, z_down = device(x, y, z + 1, core), device(x, y, z - 1, core)
    y_up, y_down = device(x, y + 1, z, core), device(x, y - 1, z, core)
    x_up, x_down = device(x + 1, y, z, core), device(x - 1, y, z, core)
    sibling = device(x, y, z, 1 - core)
    y_to = device(x, y + 1 - 2 * core, z, core)
    x_to = device(x - 1 + 2 * core, y, z, core)
    x_from = device(x + 1 - 2 * core, y, z, core)
    x_other = device(x - 1 + 2 * x_lo, y, z, core)

    row_mine = parity * half + core * quarter
    row_other = (1 - parity) * half + core * quarter
    row_sib_mine = parity * half + (1 - core) * quarter
    row_sib_other = (1 - parity) * half + (1 - core) * quarter

    def rows(k, start, size):
        return keys.at[pl.ds(pl.multiple_of(SLOT[k] * tokens + start, 16), size)]

    def z_copy(way, step):
        target = z_up if way == 0 else z_down
        k_dst = step if way == 0 else 8 - step
        k_src = step - 1 if way == 0 else (8 - (step - 1)) % 8
        start, size = row_mine, quarter
        if step == 4:
            size = quarter // 2
            start = row_mine + way * size
        if k_src == 0:
            src = kv_ref.at[pl.ds(pl.multiple_of(start, 16), size)]
        else:
            src = rows(k_src, start, size)
        return remote(src, rows(k_dst, start, size), z_send.at[way, step - 1], z_recv.at[way, step - 1], target)

    def y_copy(k, start):
        return remote(rows(k, start, quarter), rows(k, start, quarter), y_send.at[k - 1], y_recv.at[k - 1], y_to)

    def s_copy(k, which, start):
        return remote(rows(k, start, quarter), rows(k, start, quarter), s_send.at[which, k - 1], s_recv.at[which, k - 1], sibling)

    q_copy = remote(q_ref, q_far, q_send.at[0], q_recv.at[0], x_to)
    wv_copy = remote(wv_ref, wv_far, q_send.at[1], q_recv.at[1], x_to)
    back_copy = remote(back, far_out, q_send.at[2], q_recv.at[2], x_from)
    lse_copy = remote(back_lse, far_lse, q_send.at[3], q_recv.at[3], x_from)
    mine, partner = core * 2 + x_hi, core * 2 + 1 - x_hi
    wo_own = pltpu.make_async_copy(wo_ref, wo4_ref.at[mine], own_sem)
    wo_sib = remote(wo_ref, wo4_ref.at[mine], w_send.at[0], w_recv.at[0], sibling)
    wo_far = remote(wo_ref, wo4_ref.at[mine], w_send.at[1], w_recv.at[1], x_other)
    wo_fwd = remote(wo4_ref.at[partner], wo4_ref.at[partner], w_send.at[2], w_recv.at[2], sibling)

    greet([z_up, z_down, y_up, y_down, x_up, x_down, sibling])

    z_copy(0, 1).start()
    z_copy(1, 1).start()

    @pl.when(x_lo == 1)
    def _():
        q_copy.start()
        wv_copy.start()

    wo_own.start()
    wo_sib.start()
    wo_far.start()

    keys[0:tokens] = kv_ref[...]
    high[...] = jnp.full(high.shape, masked_score, F32)
    denom[...] = jnp.zeros(denom.shape, F32)
    accum[...] = jnp.zeros(accum.shape, F32)

    def tile(which, queries, slot, count, change=None):
        block = keys[slot * tokens:(slot + count) * tokens]
        chunks = [slice(0, half), slice(half, tokens)]
        scores = [dot(queries[rows_at], block, NT) for rows_at in chunks]
        for rows_at, score in zip(chunks, scores):
            if change is not None:
                score = change(score, rows_at.start)
            at = (which, rows_at, slice(None))
            old = high[at]
            new = jnp.maximum(old, jnp.max(score, axis=1, keepdims=True))
            keep = jnp.exp2((old - new) * EXP_SCALE)
            weight = jnp.exp2((score - new) * EXP_SCALE)
            denom[at] = denom[at] * keep + jnp.sum(weight, axis=1, keepdims=True)
            high[at] = new
            accum[at] = accum[at] * keep + dot(weight.astype(BF16), block[:, :latent])

    def diagonal(score, start):
        row = start + lax.broadcasted_iota(jnp.int32, score.shape, 0)
        column = lax.broadcasted_iota(jnp.int32, score.shape, 1)
        return jnp.where(column <= row, score, masked_score)

    def pair_mask(step):
        def change(score, start):
            column = lax.broadcasted_iota(jnp.int32, score.shape, 1)
            first = jnp.where(z >= step, 0, tokens)
            last = jnp.where(z + step >= 8, 2 * tokens, tokens)
            return jnp.where((column >= first) & (column < last), score, masked_score)
        return change

    def own_pair(step):
        both = (z >= step) & (z + step >= 8)
        some = (z >= step) | (z + step >= 8)

        @pl.when(both)
        def _():
            tile(0, q_ref, SLOT[step], 2)

        @pl.when(some & jnp.logical_not(both))
        def _():
            tile(0, q_ref, SLOT[step], 2, pair_mask(step))

    def far_tile(slot, count):
        @pl.when(x_lo == 0)
        def _():
            tile(1, q_far, slot, count)

    tile(0, q_ref, 0, 1, diagonal)

    def after_z(step):
        ks = [step, 8 - step] if step < 4 else [4]
        z_copy(0, step).wait_recv()
        z_copy(1, step).wait_recv()
        if step < 4:
            z_copy(0, step + 1).start()
            z_copy(1, step + 1).start()
        for k in ks:
            y_copy(k, row_mine).start()
            s_copy(k, 0, row_mine).start()

    def after_y(step):
        for k in ([step, 8 - step] if step < 4 else [4]):
            y_copy(k, row_other).wait_recv()
            s_copy(k, 1, row_other).start()

    def after_s(step):
        for k in ([step, 8 - step] if step < 4 else [4]):
            s_copy(k, 0, row_sib_mine).wait_recv()
            s_copy(k, 1, row_sib_other).wait_recv()

    after_z(1)
    after_y(1)

    @pl.when(x_lo == 0)
    def _():
        q_copy.wait_recv()
        wv_copy.wait_recv()

    far_tile(0, 1)
    after_z(2)
    after_s(1)
    own_pair(1)
    after_y(2)
    far_tile(1, 2)
    after_z(3)
    after_s(2)
    own_pair(2)
    after_y(3)
    far_tile(3, 2)
    after_z(4)
    after_s(3)
    own_pair(3)
    after_y(4)
    far_tile(5, 2)
    wo_far.wait_recv()
    wo_fwd.start()
    after_s(4)
    far_tile(7, 1)

    @pl.when(x_lo == 0)
    def _():
        latent_far = (accum[1] / denom[1]).astype(BF16)
        back[...] = dot(latent_far, wv_far[...]).astype(BF16)
        lse = high[1] * EXP_SCALE + jnp.log2(denom[1])
        back_lse[...] = jnp.broadcast_to(lse, (tokens, 128)).T[0:8]
        back_copy.start()
        lse_copy.start()

    @pl.when(z >= 4)
    def _():
        tile(0, q_ref, 7, 1)

    head_out = dot((accum[0] / denom[0]).astype(BF16), wv_ref[...])

    @pl.when(x_lo == 0)
    def _():
        out_ref[...] = head_out.astype(BF16)

    @pl.when(x_lo == 1)
    def _():
        lse = high[0] * EXP_SCALE + jnp.log2(denom[0])
        back_copy.wait_recv()
        lse_copy.wait_recv()
        other = jnp.broadcast_to(far_lse[0:1], (128, tokens)).T
        top = jnp.maximum(lse, other)
        near_part, far_part = jnp.exp2(lse - top), jnp.exp2(other - top)
        out_ref[...] = ((head_out * near_part + far_out[...].astype(F32) * far_part) / (near_part + far_part)).astype(BF16)

    wo_sib.wait_recv()
    wo_fwd.wait_recv()
    wo_own.wait()
    for copy in (wo_sib, wo_far, wo_fwd):
        copy.wait_send()
    for step in range(1, 5):
        z_copy(0, step).wait_send()
        z_copy(1, step).wait_send()
    for k in range(1, 8):
        y_copy(k, row_mine).wait_send()
        s_copy(k, 0, row_mine).wait_send()
        s_copy(k, 1, row_other).wait_send()

    @pl.when(x_lo == 1)
    def _():
        q_copy.wait_send()
        wv_copy.wait_send()

    @pl.when(x_lo == 0)
    def _():
        back_copy.wait_send()
        lse_copy.wait_send()


def attend(queries, kv, w_value, w_out):
    tokens, width = queries.shape
    latent, values = w_value.shape
    dma = pltpu.SemaphoreType.DMA
    vmem = pl.BlockSpec(memory_space=pltpu.VMEM)
    hbm = pl.BlockSpec(memory_space=pl.ANY)
    return pl.pallas_call(
        attention_kernel,
        out_shape=(
            jax.ShapeDtypeStruct((tokens, values), BF16),
            jax.ShapeDtypeStruct((4,) + w_out.shape, BF16),
        ),
        in_specs=[vmem, vmem, vmem, hbm],
        out_specs=(vmem, hbm),
        scratch_shapes=[
            pltpu.VMEM((8 * tokens, width), BF16),
            pltpu.VMEM((tokens, width), BF16),
            pltpu.VMEM((latent, values), BF16),
            pltpu.VMEM((2, tokens, 1), F32),
            pltpu.VMEM((2, tokens, 1), F32),
            pltpu.VMEM((2, tokens, latent), F32),
            pltpu.VMEM((tokens, values), BF16),
            pltpu.VMEM((8, tokens), F32),
            pltpu.VMEM((tokens, values), BF16),
            pltpu.VMEM((8, tokens), F32),
            dma((2, 4)), dma((2, 4)), dma((7,)), dma((7,)), dma((2, 7)), dma((2, 7)),
            dma((4,)), dma((4,)), dma((3,)), dma((3,)), dma,
        ],
        name="attention",
        compiler_params=pltpu.CompilerParams(collective_id=0, has_side_effects=True, vmem_limit_bytes=56 << 20),
    )(queries, kv, w_value, w_out)


def layer_kernel(
    heads_ref, wo_ref, resid_ref, gain_ref, share_ref, gate_ref, up_ref, down_ref, out_ref,
    wo, gate, up, down, pool, proj, proj_out, y_in, after, rows_in, part, sib_in, x_out, x_in,
    z_out, z_in,
    load_sem, h_send, h_recv, y_send, y_recv, az_send, az_recv, ax_send, ax_recv, as_send, as_recv,
    bs_send, bs_recv, bx_send, bx_recv, bz_send, bz_recv,
):
    x, y, z, core = coords()
    x_lo, x_hi = x % 2, x // 2
    count, width = resid_ref.shape
    piece = count // 2
    sibling = device(x, y, z, 1 - core)
    z_way = (device(x, y, z + 1, core), device(x, y, z - 1, core))
    x_to = device(x - 1 + 2 * core, y, z, core)
    x_from = device(x + 1 - 2 * core, y, z, core)
    across = device(x + 2, y, z, core)
    across_sib = device(x + 2, y, z, 1 - core)
    y_at = [device(x, y + d, z, core) for d in (1, 2, 3)]

    loads = [
        pltpu.make_async_copy(src, dst, load_sem.at[i])
        for i, (src, dst) in enumerate(((wo_ref, wo), (gate_ref, gate), (up_ref, up), (down_ref, down)))
    ]
    for load in loads:
        load.start()

    mine = core * 2 + x_hi
    head_copies = [
        remote(heads_ref.at[c_to, :, x_to_hi], pool.at[mine], h_send.at[i], h_recv.at[i], target)
        for i, (c_to, x_to_hi, target) in enumerate((
            (1 - core, x_hi, sibling), (core, 1 - x_hi, across), (1 - core, 1 - x_hi, across_sib)))
    ]
    greet([sibling, x_to, x_from, across, across_sib] + y_at + list(z_way))
    for copy in head_copies:
        copy.start()
    pool[mine] = heads_ref[core, :, x_hi]
    loads[0].wait()
    for copy in head_copies:
        copy.wait_recv()
    features = jnp.concatenate([pool[i].reshape(4 * count, pool.shape[3]) for i in range(4)], axis=1)
    attended = dot(features, wo[...].reshape(features.shape[1], width)).reshape(4, count, width)
    proj[...] = attended
    proj_out[...] = attended.astype(BF16)
    y_copies = [
        remote(proj_out.at[(y + d) % 4], y_in.at[d - 1], y_send.at[d - 1], y_recv.at[d - 1], y_at[d - 1])
        for d in (1, 2, 3)
    ]
    for copy in y_copies:
        copy.start()
    total = resid_ref[...].astype(F32) + proj[y]
    for d, copy in enumerate(y_copies):
        copy.wait_recv()
        total = total + y_in[d].astype(F32)
    after[...] = total.astype(BF16)
    widened = after[...].astype(F32)
    mean_square = jnp.mean(widened * widened, axis=1, keepdims=True)
    normed = (widened * lax.rsqrt(mean_square + norm_epsilon) * gain_ref[...]).astype(BF16)
    rows_in[0, core, 0, :, 0:width] = normed
    rows_in[0, core, 0, :, width:] = share_ref[...]

    def gather_z(way, step, chunk):
        k_dst = step if way == 0 else 8 - step
        k_src = step - 1 if way == 0 else (9 - step) % 8
        at = pl.ds(chunk * piece, piece)
        return remote(
            rows_in.at[SLOT[k_src], core, 0, at], rows_in.at[SLOT[k_dst], core, 0, at],
            az_send.at[way, step - 1, chunk], az_recv.at[way, step - 1, chunk], z_way[way])

    def gather_x(k):
        return remote(rows_in.at[SLOT[k], core, 0], rows_in.at[SLOT[k], core, 1], ax_send.at[k], ax_recv.at[k], x_to)

    def gather_s(k, column, who):
        at = rows_in.at[SLOT[k], who, column]
        return remote(at, at, as_send.at[column, k], as_recv.at[column, k], sibling)

    def return_s(slot, who):
        return remote(part.at[slot, who], sib_in.at[slot], bs_send.at[slot], bs_recv.at[slot], sibling)

    def return_x(slot):
        return remote(x_out.at[slot], x_in.at[slot], bx_send.at[slot], bx_recv.at[slot], x_from)

    def return_z(way, k, chunk):
        k_dst = k - 1 if way == 1 else (k + 1) % 8
        index = k_dst if way == 1 else (8 - k_dst) % 8
        return remote(
            z_out.at[way, index, chunk], z_in.at[way, index, chunk],
            bz_send.at[way, index, chunk], bz_recv.at[way, index, chunk], z_way[way])

    members = [[0], [1, 7], [2, 6], [3, 5], [4]]
    slots = [[SLOT[k] for k in ks] for ks in members]

    def experts(step):
        first, number = slots[step][0], len(slots[step])
        block = rows_in[first:first + number].reshape(number * 4 * count, rows_in.shape[4])
        source, shares = block[:, :width], block[:, width:].astype(F32)
        lane = lax.broadcasted_iota(jnp.int32, shares.shape, 1)
        expert = lax.axis_index("ctx")
        share = jnp.sum(jnp.where((lane == expert) | (lane == expert + 16), shares, 0.0), axis=1, keepdims=True)
        gated = dot(source, gate[...])
        hidden = (gated / (1.0 + jnp.exp(-gated)) * dot(source, up[...]) * share).astype(BF16)
        made = dot(hidden, down[...], NT).astype(BF16)
        part[first:first + number] = made.reshape(number, 2, 2, count, width)

    def send_parts(step):
        for slot in slots[step]:
            return_s(slot, 1 - core).start()

    def fold_siblings(step):
        for slot in slots[step]:
            return_s(slot, 1 - core).wait_recv()
            x_out[slot] = (part[slot, core, 1].astype(F32) + sib_in[slot, 1].astype(F32)).astype(BF16)
            return_x(slot).start()

    def after_z(step):
        for chunk in (0, 1):
            for way in (0, 1):
                if step == 4 and chunk != way:
                    continue
                gather_z(way, step, chunk).wait_recv()
                if step < 3 or (step == 3 and chunk == way):
                    gather_z(way, step + 1, chunk).start()
        for k in members[step]:
            gather_x(k).start()
            gather_s(k, 0, core).start()

    def after_x(step):
        for k in members[step]:
            gather_x(k).wait_recv()
            gather_s(k, 1, core).start()

    def after_s(step):
        for k in members[step]:
            gather_s(k, 0, 1 - core).wait_recv()
            gather_s(k, 1, 1 - core).wait_recv()

    for chunk in (0, 1):
        for way in (0, 1):
            gather_z(way, 1, chunk).start()
    gather_x(0).start()
    gather_s(0, 0, core).start()
    for load in loads[1:]:
        load.wait()
    after_x(0)
    after_s(0)
    experts(0)
    send_parts(0)
    for step in (1, 2, 3, 4):
        after_z(step)
        if step > 1:
            after_x(step - 1)
            after_s(step - 1)
            experts(step - 1)
            send_parts(step - 1)
            fold_siblings(step - 2)
    after_x(4)
    after_s(4)
    experts(4)
    send_parts(4)
    fold_siblings(3)
    fold_siblings(4)

    def local_sum(k, chunk):
        slot, at = SLOT[k], slice(chunk * piece, (chunk + 1) * piece)
        return part[slot, core, 0, at].astype(F32) + sib_in[slot, 0, at].astype(F32) + x_in[slot, at].astype(F32)

    def pass_on(way, k, chunk, incoming):
        value = local_sum(k, chunk)
        if incoming:
            index = k if way == 1 else 8 - k
            return_z(way, k + 1 if way == 1 else k - 1, chunk).wait_recv()
            value = value + z_in[way, index, chunk].astype(F32)
        copy = return_z(way, k, chunk)
        k_dst = k - 1 if way == 1 else (k + 1) % 8
        z_out[way, k_dst if way == 1 else (8 - k_dst) % 8, chunk] = value.astype(BF16)
        copy.start()

    def settle(step):
        for slot in slots[step]:
            return_x(slot).wait_recv()

    settle(4)
    pass_on(1, 4, 0, False)
    pass_on(0, 4, 1, False)
    settle(3)
    pass_on(1, 3, 1, False)
    pass_on(0, 5, 0, False)
    pass_on(1, 3, 0, True)
    pass_on(0, 5, 1, True)
    settle(2)
    for chunk in (1, 0):
        pass_on(1, 2, chunk, True)
        pass_on(0, 6, 1 - chunk, True)
    settle(1)
    for chunk in (1, 0):
        pass_on(1, 1, chunk, True)
        pass_on(0, 7, 1 - chunk, True)
    settle(0)
    for chunk in (1, 0):
        return_z(1, 1, chunk).wait_recv()
        return_z(0, 7, chunk).wait_recv()
        at = slice(chunk * piece, (chunk + 1) * piece)
        combined = local_sum(0, chunk) + z_in[1, 0, chunk].astype(F32) + z_in[0, 0, chunk].astype(F32)
        out_ref[at] = (after[at].astype(F32) + routed_factor * combined).astype(BF16)

    for copy in head_copies + y_copies:
        copy.wait_send()
    for step in (1, 2, 3, 4):
        for way in (0, 1):
            for chunk in (0, 1):
                if step < 4 or chunk == way:
                    gather_z(way, step, chunk).wait_send()
                if step < 4 or chunk != way:
                    return_z(way, step if way == 1 else 8 - step, chunk).wait_send()
    for k in range(8):
        gather_x(k).wait_send()
        gather_s(k, 0, core).wait_send()
        gather_s(k, 1, core).wait_send()
        return_s(k, 1 - core).wait_send()
        return_x(k).wait_send()


def finish_layer(head_out, w_out_part, resid, gain, share, gate, up, down):
    count, width = resid.shape
    units, values = gate.shape[1], head_out.shape[1]
    heads = head_out.reshape(2, 4, 2, count, values)
    dma = pltpu.SemaphoreType.DMA
    vmem = pl.BlockSpec(memory_space=pltpu.VMEM)
    hbm = pl.BlockSpec(memory_space=pl.ANY)
    return pl.pallas_call(
        layer_kernel,
        out_shape=jax.ShapeDtypeStruct((count, width), BF16),
        in_specs=[vmem, hbm, vmem, vmem, vmem, hbm, hbm, hbm],
        out_specs=vmem,
        scratch_shapes=[
            pltpu.VMEM(w_out_part.shape, BF16),
            pltpu.VMEM((width, units), BF16),
            pltpu.VMEM((width, units), BF16),
            pltpu.VMEM((width, units), BF16),
            pltpu.VMEM((4, 4, count, values), BF16),
            pltpu.VMEM((4, count, width), F32),
            pltpu.VMEM((4, count, width), BF16),
            pltpu.VMEM((3, count, width), BF16),
            pltpu.VMEM((count, width), BF16),
            pltpu.VMEM((8, 2, 2, count, width + 128), BF16),
            pltpu.VMEM((8, 2, 2, count, width), BF16),
            pltpu.VMEM((8, 2, count, width), BF16),
            pltpu.VMEM((8, count, width), BF16),
            pltpu.VMEM((8, count, width), BF16),
            pltpu.VMEM((2, 4, 2, count // 2, width), BF16),
            pltpu.VMEM((2, 4, 2, count // 2, width), BF16),
            dma((4,)), dma((3,)), dma((3,)), dma((3,)), dma((3,)),
            dma((2, 4, 2)), dma((2, 4, 2)), dma((8,)), dma((8,)), dma((2, 8)), dma((2, 8)),
            dma((8,)), dma((8,)), dma((8,)), dma((8,)), dma((2, 4, 2)), dma((2, 4, 2)),
        ],
        name="layer",
        compiler_params=pltpu.CompilerParams(collective_id=1, has_side_effects=True, vmem_limit_bytes=60 << 20),
    )(heads, w_out_part, resid, gain.reshape(1, width), share, gate, up, down)


def routing_shares(expert_ids, route_scores, experts):
    combine = route_scores / jnp.sum(route_scores, axis=1, keepdims=True)
    named = expert_ids[:, :, None] == jnp.arange(experts, dtype=jnp.int32)[None, None, :]
    dense = jnp.sum(jnp.where(named, combine[:, :, None], 0.0), axis=1)
    coarse = lax.reduce_precision(dense, 8, 7)
    pieces = jnp.concatenate([coarse, dense - coarse], axis=1).astype(BF16)
    return jnp.pad(pieces, ((0, 0), (0, 128 - 2 * experts)))


def per_device(
    q_latent,
    kv_latent,
    w_value,
    w_out,
    resid,
    norm_gain,
    w_gate,
    w_up,
    w_down_t,
    expert_ids,
    route_scores,
):
    head_out, w_out_part = attend(
        q_latent.reshape(q_latent.shape[0], q_latent.shape[2]), kv_latent, w_value[0], w_out
    )
    share = routing_shares(expert_ids, route_scores, lax.axis_size("ctx"))
    return finish_layer(
        head_out, w_out_part, resid, norm_gain, share, w_gate[0], w_up[0], w_down_t[0]
    )


def solution(mesh):
    placed = (
        P("ctx", ("head", "ep"), None),
        P("ctx", None),
        P(("head", "ep"), None, None),
        P(("head", "ep"), None),
        P(("ctx", "head", "ep"), None),
        P(),
        P("ctx", None, "head"),
        P("ctx", None, "head"),
        P("ctx", None, "head"),
        P(("ctx", "head", "ep"), None),
        P(("ctx", "head", "ep"), None),
    )
    return jax.shard_map(
        per_device,
        mesh=mesh,
        in_specs=placed,
        out_specs=P(("ctx", "head", "ep"), None),
        check_vma=False,
    )
```

```python
import jax
import jax.numpy as jnp
from jax import lax
from jax.experimental import pallas as pl
from jax.experimental.pallas import tpu as pltpu
from jax.sharding import PartitionSpec as P

MESH = pl.DeviceIdType.MESH
BF16, F32 = jnp.bfloat16, jnp.float32
NT = (((1,), (1,)), ((), ()))
NN = (((1,), (0,)), ((), ()))
ROPE = 64
NOPE = 128
TOPK = 6
LOG2E = 1.4426950408889634
EXP_SCALE = (NOPE + ROPE) ** (-0.5) * LOG2E
routed_factor = 2.446
norm_epsilon = 1e-06
masked_score = -1e30


def dot(a, b, dims=NN):
    return lax.dot_general(a, b, dims, preferred_element_type=F32)


def coords():
    ctx, core, ep = lax.axis_index("ctx"), lax.axis_index("head"), lax.axis_index("ep")
    x_lo, z, y, x_hi = ctx // 8, ctx % 8, ep // 2, ep % 2
    return x_hi * 2 + x_lo, y, z, core


def device(x, y, z, core):
    x, y, z = (x + 4) % 4, (y + 4) % 4, (z + 8) % 8
    return ((x % 2) * 8 + z, core, y * 2 + x // 2)


def greet(partners):
    barrier = pltpu.get_barrier_semaphore()
    for partner in partners:
        pl.semaphore_signal(barrier, inc=1, device_id=partner, device_id_type=MESH)
    pl.semaphore_wait(barrier, len(partners))


def remote(src, dst, send_sem, recv_sem, target):
    return pltpu.make_async_remote_copy(
        src_ref=src, dst_ref=dst, send_sem=send_sem, recv_sem=recv_sem,
        device_id=target, device_id_type=MESH,
    )


SLOT = {0: 0, 1: 1, 7: 2, 2: 3, 6: 4, 3: 5, 5: 6, 4: 7}


def attention_kernel(
    q_ref, kv_ref, wv_ref, wo_ref, out_ref, wo4_ref,
    keys, q_far, queries, wv_far, high, denom, accum, back, back_lse, far_out, far_lse,
    z_send, z_recv, y_send, y_recv, s_send, s_recv, q_send, q_recv, w_send, w_recv, own_sem,
):
    x, y, z, core = coords()
    x_lo, x_hi, parity = x % 2, x // 2, y % 2
    tokens, latent = q_ref.shape[1], wv_ref.shape[0]
    half, quarter, piece = tokens // 2, tokens // 4, q_ref.shape[0] // 2
    z_way = (device(x, y, z + 1, core), device(x, y, z - 1, core))
    y_up, y_down = device(x, y + 1, z, core), device(x, y - 1, z, core)
    x_up, x_down = device(x + 1, y, z, core), device(x - 1, y, z, core)
    sibling = device(x, y, z, 1 - core)
    y_to = device(x, y + 1 - 2 * core, z, core)
    x_to = device(x - 1 + 2 * core, y, z, core)
    x_from = device(x + 1 - 2 * core, y, z, core)
    x_other = device(x - 1 + 2 * x_lo, y, z, core)

    mine, other = parity * 2 + core, (1 - parity) * 2 + core
    sib_mine, sib_other = parity * 2 + 1 - core, (1 - parity) * 2 + 1 - core

    def z_copy(way, step, chunk):
        k_dst = step if way == 0 else 8 - step
        k_src = step - 1 if way == 0 else (9 - step) % 8
        at = pl.ds(chunk * piece, piece)
        return remote(
            keys.at[SLOT[k_src], mine, at], keys.at[SLOT[k_dst], mine, at],
            z_send.at[way, step - 1, chunk], z_recv.at[way, step - 1, chunk], z_way[way])

    def y_copy(k, which):
        at = keys.at[SLOT[k], which]
        return remote(at, at, y_send.at[k - 1], y_recv.at[k - 1], y_to)

    def s_copy(k, row, which):
        at = keys.at[SLOT[k], which]
        return remote(at, at, s_send.at[row, k - 1], s_recv.at[row, k - 1], sibling)

    q_copy = remote(q_ref, q_far, q_send.at[0], q_recv.at[0], x_to)
    wv_copy = remote(wv_ref, wv_far, q_send.at[1], q_recv.at[1], x_to)
    back_copy = remote(back, far_out, q_send.at[2], q_recv.at[2], x_from)
    lse_copy = remote(back_lse, far_lse, q_send.at[3], q_recv.at[3], x_from)
    place, partner = core * 2 + x_hi, core * 2 + 1 - x_hi
    wo_own = pltpu.make_async_copy(wo_ref, wo4_ref.at[place], own_sem)
    wo_sib = remote(wo_ref, wo4_ref.at[place], w_send.at[0], w_recv.at[0], sibling)
    wo_far = remote(wo_ref, wo4_ref.at[place], w_send.at[1], w_recv.at[1], x_other)
    wo_fwd = remote(wo4_ref.at[partner], wo4_ref.at[partner], w_send.at[2], w_recv.at[2], sibling)

    for j in range(4):
        keys[0, j] = kv_ref[:, j * quarter:(j + 1) * quarter]
    greet([*z_way, y_up, y_down, x_up, x_down, sibling])

    for chunk in (0, 1):
        for way in (0, 1):
            z_copy(way, 1, chunk).start()

    @pl.when(x_lo == 1)
    def _():
        q_copy.start()
        wv_copy.start()

    wo_own.start()
    wo_sib.start()
    wo_far.start()

    queries[0] = q_ref[...].T
    high[...] = jnp.full(high.shape, masked_score, F32)
    denom[...] = jnp.zeros(denom.shape, F32)
    accum[...] = jnp.zeros(accum.shape, F32)

    def tile(which, slot, count, change=None):
        block = jnp.concatenate([keys[slot + i, j] for i in range(count) for j in range(4)], axis=1)
        chunks = [slice(0, half), slice(half, tokens)]
        scores = [dot(queries[which, rows_at], block) for rows_at in chunks]
        for rows_at, score in zip(chunks, scores):
            if change is not None:
                score = change(score, rows_at.start)
            at = (which, rows_at, slice(None))
            old = high[at]
            new = jnp.maximum(old, jnp.max(score, axis=1, keepdims=True))
            keep = jnp.exp2((old - new) * EXP_SCALE)
            weight = jnp.exp2((score - new) * EXP_SCALE)
            denom[at] = denom[at] * keep + jnp.sum(weight, axis=1, keepdims=True)
            high[at] = new
            accum[at] = accum[at] * keep + dot(weight.astype(BF16), block[:latent], NT)

    def diagonal(score, start):
        row = start + lax.broadcasted_iota(jnp.int32, score.shape, 0)
        column = lax.broadcasted_iota(jnp.int32, score.shape, 1)
        return jnp.where(column <= row, score, masked_score)

    def pair_mask(step):
        def change(score, start):
            column = lax.broadcasted_iota(jnp.int32, score.shape, 1)
            first = jnp.where(z >= step, 0, tokens)
            last = jnp.where(z + step >= 8, 2 * tokens, tokens)
            return jnp.where((column >= first) & (column < last), score, masked_score)
        return change

    def own_pair(step):
        both = (z >= step) & (z + step >= 8)
        some = (z >= step) | (z + step >= 8)

        @pl.when(both)
        def _():
            tile(0, SLOT[step], 2)

        @pl.when(some & jnp.logical_not(both))
        def _():
            tile(0, SLOT[step], 2, pair_mask(step))

    def far_tile(slot, count):
        @pl.when(x_lo == 0)
        def _():
            tile(1, slot, count)

    members = {1: [1, 7], 2: [2, 6], 3: [3, 5], 4: [4]}

    def after_z(step, chunk):
        for way in (0, 1):
            if step < 4 or chunk == way:
                z_copy(way, step, chunk).wait_recv()
                if step < 3 or (step == 3 and chunk == way):
                    z_copy(way, step + 1, chunk).start()

    def share_z(step):
        for k in members[step]:
            y_copy(k, mine).start()
            s_copy(k, 0, mine).start()

    def after_y(step):
        for k in members[step]:
            y_copy(k, other).wait_recv()
            s_copy(k, 1, other).start()

    def after_s(step):
        for k in members[step]:
            s_copy(k, 0, sib_mine).wait_recv()
            s_copy(k, 1, sib_other).wait_recv()

    tile(0, 0, 1, diagonal)
    after_z(1, 0)
    after_z(1, 1)
    share_z(1)

    @pl.when(x_lo == 0)
    def _():
        q_copy.wait_recv()
        wv_copy.wait_recv()
        queries[1] = q_far[...].T

    after_z(2, 0)
    after_y(1)
    far_tile(0, 1)
    after_z(2, 1)
    share_z(2)
    after_s(1)
    own_pair(1)
    after_z(3, 0)
    after_y(2)
    far_tile(1, 2)
    after_z(3, 1)
    share_z(3)
    after_s(2)
    own_pair(2)
    after_z(4, 0)
    after_z(4, 1)
    share_z(4)
    after_y(3)
    far_tile(3, 2)
    after_s(3)
    after_y(4)
    own_pair(3)
    wo_far.wait_recv()
    wo_fwd.start()
    far_tile(5, 2)
    after_s(4)
    far_tile(7, 1)

    @pl.when(x_lo == 0)
    def _():
        latent_far = (accum[1] / denom[1]).astype(BF16)
        back[...] = dot(latent_far, wv_far[...]).astype(BF16)
        lse = high[1] * EXP_SCALE + jnp.log2(denom[1])
        back_lse[...] = jnp.broadcast_to(lse, (tokens, 128)).T[0:8]
        back_copy.start()
        lse_copy.start()

    @pl.when(z >= 4)
    def _():
        tile(0, 7, 1)

    head_out = dot((accum[0] / denom[0]).astype(BF16), wv_ref[...])

    @pl.when(x_lo == 0)
    def _():
        out_ref[...] = head_out.astype(BF16)

    @pl.when(x_lo == 1)
    def _():
        lse = high[0] * EXP_SCALE + jnp.log2(denom[0])
        back_copy.wait_recv()
        lse_copy.wait_recv()
        far = jnp.broadcast_to(far_lse[0:1], (128, tokens)).T
        top = jnp.maximum(lse, far)
        near_part, far_part = jnp.exp2(lse - top), jnp.exp2(far - top)
        out_ref[...] = ((head_out * near_part + far_out[...].astype(F32) * far_part) / (near_part + far_part)).astype(BF16)

    wo_sib.wait_recv()
    wo_fwd.wait_recv()
    wo_own.wait()
    for copy in (wo_sib, wo_far, wo_fwd):
        copy.wait_send()
    for step in range(1, 5):
        for way in (0, 1):
            for chunk in (0, 1):
                if step < 4 or chunk == way:
                    z_copy(way, step, chunk).wait_send()
    for k in range(1, 8):
        y_copy(k, mine).wait_send()
        s_copy(k, 0, mine).wait_send()
        s_copy(k, 1, other).wait_send()

    @pl.when(x_lo == 1)
    def _():
        q_copy.wait_send()
        wv_copy.wait_send()

    @pl.when(x_lo == 0)
    def _():
        back_copy.wait_send()
        lse_copy.wait_send()


def attend(queries, kv, w_value, w_out):
    width, tokens = queries.shape
    latent, values = w_value.shape
    dma = pltpu.SemaphoreType.DMA
    vmem = pl.BlockSpec(memory_space=pltpu.VMEM)
    hbm = pl.BlockSpec(memory_space=pl.ANY)
    return pl.pallas_call(
        attention_kernel,
        out_shape=(
            jax.ShapeDtypeStruct((tokens, values), BF16),
            jax.ShapeDtypeStruct((4,) + w_out.shape, BF16),
        ),
        in_specs=[vmem, vmem, vmem, hbm],
        out_specs=(vmem, hbm),
        scratch_shapes=[
            pltpu.VMEM((8, 4, width, tokens // 4), BF16),
            pltpu.VMEM((width, tokens), BF16),
            pltpu.VMEM((2, tokens, width), BF16),
            pltpu.VMEM((latent, values), BF16),
            pltpu.VMEM((2, tokens, 1), F32),
            pltpu.VMEM((2, tokens, 1), F32),
            pltpu.VMEM((2, tokens, latent), F32),
            pltpu.VMEM((tokens, values), BF16),
            pltpu.VMEM((8, tokens), F32),
            pltpu.VMEM((tokens, values), BF16),
            pltpu.VMEM((8, tokens), F32),
            dma((2, 4, 2)), dma((2, 4, 2)), dma((7,)), dma((7,)), dma((2, 7)), dma((2, 7)),
            dma((4,)), dma((4,)), dma((3,)), dma((3,)), dma,
        ],
        name="attention",
        compiler_params=pltpu.CompilerParams(collective_id=0, has_side_effects=True, vmem_limit_bytes=56 << 20),
    )(queries, kv, w_value, w_out)


def routing_shares(ids_ref, scores_ref, experts):
    scores = scores_ref[...]
    combine = scores / jnp.sum(scores, axis=0, keepdims=True)
    lane = lax.broadcasted_iota(jnp.int32, (128, scores.shape[1]), 0)
    dense = jnp.zeros((128, scores.shape[1]), F32)
    for k in range(scores.shape[0]):
        chosen = ids_ref[k:k + 1]
        dense += jnp.where((lane == chosen) | (lane == chosen + experts), combine[k:k + 1], 0.0)
    coarse = dense.astype(BF16).astype(F32)
    return jnp.where(lane < experts, coarse, dense - coarse).T


def layer_kernel(
    heads_ref, wo_ref, resid_ref, gain_ref, ids_ref, scores_ref, gate_ref, up_ref, down_ref, out_ref,
    wo, gate, up, down, pool, proj, proj_out, y_in, after, rows_in, part, hidden, sib_in, x_out, x_in,
    z_out, z_in,
    load_sem, h_send, h_recv, y_send, y_recv, az_send, az_recv, ax_send, ax_recv, as_send, as_recv,
    bs_send, bs_recv, bx_send, bx_recv, bz_send, bz_recv,
):
    x, y, z, core = coords()
    x_lo, x_hi = x % 2, x // 2
    count, width = resid_ref.shape
    piece = count // 2
    sibling = device(x, y, z, 1 - core)
    z_way = (device(x, y, z + 1, core), device(x, y, z - 1, core))
    x_to = device(x - 1 + 2 * core, y, z, core)
    x_from = device(x + 1 - 2 * core, y, z, core)
    across = device(x + 2, y, z, core)
    across_sib = device(x + 2, y, z, 1 - core)
    y_at = [device(x, y + d, z, core) for d in (1, 2, 3)]

    loads = [
        pltpu.make_async_copy(src, dst, load_sem.at[i])
        for i, (src, dst) in enumerate(((wo_ref, wo), (gate_ref, gate), (up_ref, up), (down_ref, down)))
    ]
    for load in loads:
        load.start()

    mine = core * 2 + x_hi
    head_copies = [
        remote(heads_ref.at[c_to, :, x_to_hi], pool.at[mine], h_send.at[i], h_recv.at[i], target)
        for i, (c_to, x_to_hi, target) in enumerate((
            (1 - core, x_hi, sibling), (core, 1 - x_hi, across), (1 - core, 1 - x_hi, across_sib)))
    ]
    greet([sibling, x_to, x_from, across, across_sib] + y_at + list(z_way))
    for copy in head_copies:
        copy.start()
    pool[mine] = heads_ref[core, :, x_hi]
    loads[0].wait()
    for copy in head_copies:
        copy.wait_recv()
    features = jnp.concatenate([pool[i].reshape(4 * count, pool.shape[3]) for i in range(4)], axis=1)
    attended = dot(features, wo[...].reshape(features.shape[1], width)).reshape(4, count, width)
    proj[...] = attended
    proj_out[...] = attended.astype(BF16)
    y_copies = [
        remote(proj_out.at[(y + d) % 4], y_in.at[d - 1], y_send.at[d - 1], y_recv.at[d - 1], y_at[d - 1])
        for d in (1, 2, 3)
    ]
    for copy in y_copies:
        copy.start()
    total = resid_ref[...].astype(F32) + proj[y]
    for d, copy in enumerate(y_copies):
        copy.wait_recv()
        total = total + y_in[d].astype(F32)
    after[...] = total.astype(BF16)
    widened = after[...].astype(F32)
    mean_square = jnp.mean(widened * widened, axis=1, keepdims=True)
    normed = (widened * lax.rsqrt(mean_square + norm_epsilon) * gain_ref[...]).astype(BF16)
    rows_in[0, core, 0, :, 0:width] = normed
    rows_in[0, core, 0, :, width:] = routing_shares(ids_ref, scores_ref, 16).astype(BF16)

    def gather_z(way, step, chunk):
        k_dst = step if way == 0 else 8 - step
        k_src = step - 1 if way == 0 else (9 - step) % 8
        at = pl.ds(chunk * piece, piece)
        return remote(
            rows_in.at[SLOT[k_src], core, 0, at], rows_in.at[SLOT[k_dst], core, 0, at],
            az_send.at[way, step - 1, chunk], az_recv.at[way, step - 1, chunk], z_way[way])

    def gather_x(k):
        return remote(rows_in.at[SLOT[k], core, 0], rows_in.at[SLOT[k], core, 1], ax_send.at[k], ax_recv.at[k], x_to)

    def gather_s(k, column, who):
        at = rows_in.at[SLOT[k], who, column]
        return remote(at, at, as_send.at[column, k], as_recv.at[column, k], sibling)

    def return_s(slot, who):
        return remote(part.at[slot, who], sib_in.at[slot], bs_send.at[slot], bs_recv.at[slot], sibling)

    def return_x(slot):
        return remote(x_out.at[slot], x_in.at[slot], bx_send.at[slot], bx_recv.at[slot], x_from)

    def return_z(way, k, chunk):
        k_dst = k - 1 if way == 1 else (k + 1) % 8
        index = k_dst if way == 1 else (8 - k_dst) % 8
        return remote(
            z_out.at[way, index, chunk], z_in.at[way, index, chunk],
            bz_send.at[way, index, chunk], bz_recv.at[way, index, chunk], z_way[way])

    members = [[0], [1, 7], [2, 6], [3, 5], [4]]
    slots = [[SLOT[k] for k in ks] for ks in members]

    def hidden_units(step):
        first, number = slots[step][0], len(slots[step])
        block = rows_in[first:first + number].reshape(number * 4 * count, rows_in.shape[4])
        source, shares = block[:, :width], block[:, width:].astype(F32)
        lane = lax.broadcasted_iota(jnp.int32, shares.shape, 1)
        expert = lax.axis_index("ctx")
        share = jnp.sum(jnp.where((lane == expert) | (lane == expert + 16), shares, 0.0), axis=1, keepdims=True)
        gated = dot(source, gate[...], NT)
        value = gated / (1.0 + jnp.exp(-gated)) * dot(source, up[...], NT) * share
        hidden[0:number * 4 * count] = value.astype(BF16)

    def project_down(step):
        first, number = slots[step][0], len(slots[step])
        made = dot(hidden[0:number * 4 * count], down[...]).astype(BF16)
        part[first:first + number] = made.reshape(number, 2, 2, count, width)
        for slot in slots[step]:
            return_s(slot, 1 - core).start()

    def fold_siblings(step):
        for slot in slots[step]:
            return_s(slot, 1 - core).wait_recv()
            x_out[slot] = (part[slot, core, 1].astype(F32) + sib_in[slot, 1].astype(F32)).astype(BF16)
            return_x(slot).start()

    def after_z(step, chunk):
        for way in (0, 1):
            if step < 4 or chunk == way:
                gather_z(way, step, chunk).wait_recv()
                if step < 3 or (step == 3 and chunk == way):
                    gather_z(way, step + 1, chunk).start()

    def share_z(step):
        for k in members[step]:
            gather_x(k).start()
            gather_s(k, 0, core).start()

    def after_x(step):
        for k in members[step]:
            gather_x(k).wait_recv()
            gather_s(k, 1, core).start()

    def after_s(step):
        for k in members[step]:
            gather_s(k, 0, 1 - core).wait_recv()
            gather_s(k, 1, 1 - core).wait_recv()

    for chunk in (0, 1):
        for way in (0, 1):
            gather_z(way, 1, chunk).start()
    gather_x(0).start()
    gather_s(0, 0, core).start()
    for load in loads[1:]:
        load.wait()
    after_z(1, 0)
    after_z(1, 1)
    share_z(1)
    after_x(0)
    after_s(0)
    hidden_units(0)
    after_z(2, 0)
    project_down(0)
    after_z(2, 1)
    share_z(2)
    after_x(1)
    after_z(3, 0)
    after_s(1)
    fold_siblings(0)
    hidden_units(1)
    after_z(3, 1)
    share_z(3)
    project_down(1)
    after_z(4, 0)
    after_z(4, 1)
    share_z(4)
    after_x(2)
    after_s(2)
    hidden_units(2)
    after_x(3)
    fold_siblings(1)
    project_down(2)
    after_s(3)
    hidden_units(3)
    after_x(4)
    fold_siblings(2)
    project_down(3)
    after_s(4)
    hidden_units(4)
    fold_siblings(3)
    project_down(4)

    def local_sum(k, chunk):
        slot, at = SLOT[k], slice(chunk * piece, (chunk + 1) * piece)
        return part[slot, core, 0, at].astype(F32) + sib_in[slot, 0, at].astype(F32) + x_in[slot, at].astype(F32)

    def pass_on(way, k, chunk, incoming):
        value = local_sum(k, chunk)
        if incoming:
            index = k if way == 1 else 8 - k
            return_z(way, k + 1 if way == 1 else k - 1, chunk).wait_recv()
            value = value + z_in[way, index, chunk].astype(F32)
        copy = return_z(way, k, chunk)
        k_dst = k - 1 if way == 1 else (k + 1) % 8
        z_out[way, k_dst if way == 1 else (8 - k_dst) % 8, chunk] = value.astype(BF16)
        copy.start()

    def settle(step):
        for slot in slots[step]:
            return_x(slot).wait_recv()

    settle(3)
    pass_on(1, 3, 1, False)
    pass_on(0, 5, 0, False)
    fold_siblings(4)
    settle(4)
    pass_on(1, 4, 0, False)
    pass_on(0, 4, 1, False)
    pass_on(1, 3, 0, True)
    pass_on(0, 5, 1, True)
    settle(2)
    for chunk in (1, 0):
        pass_on(1, 2, chunk, True)
        pass_on(0, 6, 1 - chunk, True)
    settle(1)
    for chunk in (1, 0):
        pass_on(1, 1, chunk, True)
        pass_on(0, 7, 1 - chunk, True)
    settle(0)
    for chunk in (1, 0):
        return_z(1, 1, chunk).wait_recv()
        return_z(0, 7, chunk).wait_recv()
        at = slice(chunk * piece, (chunk + 1) * piece)
        combined = local_sum(0, chunk) + z_in[1, 0, chunk].astype(F32) + z_in[0, 0, chunk].astype(F32)
        out_ref[at] = (after[at].astype(F32) + routed_factor * combined).astype(BF16)

    for copy in head_copies + y_copies:
        copy.wait_send()
    for step in (1, 2, 3, 4):
        for way in (0, 1):
            for chunk in (0, 1):
                if step < 4 or chunk == way:
                    gather_z(way, step, chunk).wait_send()
                if step < 4 or chunk != way:
                    return_z(way, step if way == 1 else 8 - step, chunk).wait_send()
    for k in range(8):
        gather_x(k).wait_send()
        gather_s(k, 0, core).wait_send()
        gather_s(k, 1, core).wait_send()
        return_s(k, 1 - core).wait_send()
        return_x(k).wait_send()


def finish_layer(head_out, w_out_part, resid, gain, ids, scores, gate, up, down):
    count, width = resid.shape
    units, values = gate.shape[0], head_out.shape[1]
    heads = head_out.reshape(2, 4, 2, count, values)
    dma = pltpu.SemaphoreType.DMA
    vmem = pl.BlockSpec(memory_space=pltpu.VMEM)
    hbm = pl.BlockSpec(memory_space=pl.ANY)
    return pl.pallas_call(
        layer_kernel,
        out_shape=jax.ShapeDtypeStruct((count, width), BF16),
        in_specs=[vmem, hbm, vmem, vmem, vmem, vmem, hbm, hbm, hbm],
        out_specs=vmem,
        scratch_shapes=[
            pltpu.VMEM(w_out_part.shape, BF16),
            pltpu.VMEM((units, width), BF16),
            pltpu.VMEM((units, width), BF16),
            pltpu.VMEM((units, width), BF16),
            pltpu.VMEM((4, 4, count, values), BF16),
            pltpu.VMEM((4, count, width), F32),
            pltpu.VMEM((4, count, width), BF16),
            pltpu.VMEM((3, count, width), BF16),
            pltpu.VMEM((count, width), BF16),
            pltpu.VMEM((8, 2, 2, count, width + 128), BF16),
            pltpu.VMEM((8, 2, 2, count, width), BF16),
            pltpu.VMEM((8 * count, units), BF16),
            pltpu.VMEM((8, 2, count, width), BF16),
            pltpu.VMEM((8, count, width), BF16),
            pltpu.VMEM((8, count, width), BF16),
            pltpu.VMEM((2, 4, 2, count // 2, width), BF16),
            pltpu.VMEM((2, 4, 2, count // 2, width), BF16),
            dma((4,)), dma((3,)), dma((3,)), dma((3,)), dma((3,)),
            dma((2, 4, 2)), dma((2, 4, 2)), dma((8,)), dma((8,)), dma((2, 8)), dma((2, 8)),
            dma((8,)), dma((8,)), dma((8,)), dma((8,)), dma((2, 4, 2)), dma((2, 4, 2)),
        ],
        name="layer",
        compiler_params=pltpu.CompilerParams(collective_id=1, has_side_effects=True, vmem_limit_bytes=60 << 20),
    )(heads, w_out_part, resid, gain.reshape(1, width), ids, scores, gate, up, down)


def per_device(
    q_latent,
    kv_latent,
    w_value,
    w_out,
    resid,
    norm_gain,
    w_gate,
    w_up,
    w_down_t,
    expert_ids,
    route_scores,
):
    head_out, w_out_part = attend(
        q_latent.reshape(q_latent.shape[0], q_latent.shape[2]).T, kv_latent.T, w_value[0], w_out
    )
    return finish_layer(
        head_out, w_out_part, resid, norm_gain, expert_ids.T, route_scores.T, w_gate[0].T, w_up[0].T, w_down_t[0].T
    )


def solution(mesh):
    placed = (
        P("ctx", ("head", "ep"), None),
        P("ctx", None),
        P(("head", "ep"), None, None),
        P(("head", "ep"), None),
        P(("ctx", "head", "ep"), None),
        P(),
        P("ctx", None, "head"),
        P("ctx", None, "head"),
        P("ctx", None, "head"),
        P(("ctx", "head", "ep"), None),
        P(("ctx", "head", "ep"), None),
    )
    return jax.shard_map(
        per_device,
        mesh=mesh,
        in_specs=placed,
        out_specs=P(("ctx", "head", "ep"), None),
        check_vma=False,
    )
```

```python
import jax
import jax.numpy as jnp
from jax import lax
from jax.experimental import pallas as pl
from jax.experimental.pallas import tpu as pltpu
from jax.sharding import PartitionSpec as P

MESH = pl.DeviceIdType.MESH
BF16, F32 = jnp.bfloat16, jnp.float32
NT = (((1,), (1,)), ((), ()))
NN = (((1,), (0,)), ((), ()))
ROPE = 64
NOPE = 128
TOPK = 6
LOG2E = 1.4426950408889634
EXP_SCALE = (NOPE + ROPE) ** (-0.5) * LOG2E
routed_factor = 2.446
norm_epsilon = 1e-06
masked_score = -1e30


def dot(a, b, dims=NN):
    return lax.dot_general(a, b, dims, preferred_element_type=F32)


def coords():
    ctx, core, ep = lax.axis_index("ctx"), lax.axis_index("head"), lax.axis_index("ep")
    x_lo, z, y, x_hi = ctx // 8, ctx % 8, ep // 2, ep % 2
    return x_hi * 2 + x_lo, y, z, core


def device(x, y, z, core):
    x, y, z = (x + 4) % 4, (y + 4) % 4, (z + 8) % 8
    return ((x % 2) * 8 + z, core, y * 2 + x // 2)


def greet(partners):
    barrier = pltpu.get_barrier_semaphore()
    for partner in partners:
        pl.semaphore_signal(barrier, inc=1, device_id=partner, device_id_type=MESH)
    pl.semaphore_wait(barrier, len(partners))


def remote(src, dst, send_sem, recv_sem, target):
    return pltpu.make_async_remote_copy(
        src_ref=src, dst_ref=dst, send_sem=send_sem, recv_sem=recv_sem,
        device_id=target, device_id_type=MESH,
    )


SLOT = {0: 0, 1: 1, 7: 2, 2: 3, 6: 4, 3: 5, 5: 6, 4: 7}


def attention_part(
    q_ref, kv_ref, wv_ref, wo_ref, heads, wo4_ref,
    keys, q_far, queries, wv_far, high, denom, accum, back, back_lse, far_out, far_lse,
    z_send, z_recv, y_send, y_recv, s_send, s_recv, q_send, q_recv, w_send, w_recv, own_sem,
):
    x, y, z, core = coords()
    x_lo, x_hi, parity = x % 2, x // 2, y % 2
    tokens, latent = q_ref.shape[1], wv_ref.shape[0]
    half, quarter, piece = tokens // 2, tokens // 4, q_ref.shape[0] // 2
    z_way = (device(x, y, z + 1, core), device(x, y, z - 1, core))
    y_up, y_down = device(x, y + 1, z, core), device(x, y - 1, z, core)
    x_up, x_down = device(x + 1, y, z, core), device(x - 1, y, z, core)
    sibling = device(x, y, z, 1 - core)
    y_to = device(x, y + 1 - 2 * core, z, core)
    x_to = device(x - 1 + 2 * core, y, z, core)
    x_from = device(x + 1 - 2 * core, y, z, core)
    x_other = device(x - 1 + 2 * x_lo, y, z, core)

    mine, other = parity * 2 + core, (1 - parity) * 2 + core
    sib_mine, sib_other = parity * 2 + 1 - core, (1 - parity) * 2 + 1 - core

    def z_copy(way, step, chunk):
        k_dst = step if way == 0 else 8 - step
        k_src = step - 1 if way == 0 else (9 - step) % 8
        at = pl.ds(chunk * piece, piece)
        return remote(
            keys.at[SLOT[k_src], mine, at], keys.at[SLOT[k_dst], mine, at],
            z_send.at[way, step - 1, chunk], z_recv.at[way, step - 1, chunk], z_way[way])

    def y_copy(k, which, chunk):
        at = keys.at[SLOT[k], which, pl.ds(chunk * piece, piece)]
        return remote(at, at, y_send.at[k - 1, chunk], y_recv.at[k - 1, chunk], y_to)

    def s_copy(k, row, which, chunk):
        at = keys.at[SLOT[k], which, pl.ds(chunk * piece, piece)]
        return remote(at, at, s_send.at[row, k - 1, chunk], s_recv.at[row, k - 1, chunk], sibling)

    q_copy = remote(q_ref, q_far, q_send.at[0], q_recv.at[0], x_to)
    wv_copy = remote(wv_ref, wv_far, q_send.at[1], q_recv.at[1], x_to)
    back_copy = remote(back, far_out, q_send.at[2], q_recv.at[2], x_from)
    lse_copy = remote(back_lse, far_lse, q_send.at[3], q_recv.at[3], x_from)
    place, partner = core * 2 + x_hi, core * 2 + 1 - x_hi
    wo_own = pltpu.make_async_copy(wo_ref, wo4_ref.at[place], own_sem)
    wo_sib = remote(wo_ref, wo4_ref.at[place], w_send.at[0], w_recv.at[0], sibling)
    wo_far = remote(wo_ref, wo4_ref.at[place], w_send.at[1], w_recv.at[1], x_other)
    wo_fwd = remote(wo4_ref.at[partner], wo4_ref.at[partner], w_send.at[2], w_recv.at[2], sibling)

    for j in range(4):
        keys[0, j] = kv_ref[:, j * quarter:(j + 1) * quarter]
    greet([*z_way, y_up, y_down, device(x, y + 2, z, core), x_up, x_down, sibling,
           device(x + 2, y, z, core), device(x + 2, y, z, 1 - core)])

    for chunk in (0, 1):
        for way in (0, 1):
            z_copy(way, 1, chunk).start()

    @pl.when(x_lo == 1)
    def _():
        q_copy.start()
        wv_copy.start()

    wo_own.start()
    wo_sib.start()
    wo_far.start()

    queries[0] = q_ref[...].T
    high[...] = jnp.full(high.shape, masked_score, F32)
    denom[...] = jnp.zeros(denom.shape, F32)
    accum[...] = jnp.zeros(accum.shape, F32)

    def tile(which, slot, count, change=None):
        block = jnp.concatenate([keys[slot + i, j] for i in range(count) for j in range(4)], axis=1)
        chunks = [slice(0, half), slice(half, tokens)]
        scores = [dot(queries[which, rows_at], block) for rows_at in chunks]
        for rows_at, score in zip(chunks, scores):
            if change is not None:
                score = change(score, rows_at.start)
            at = (which, rows_at, slice(None))
            old = high[at]
            new = jnp.maximum(old, jnp.max(score, axis=1, keepdims=True))
            keep = jnp.exp2((old - new) * EXP_SCALE)
            weight = jnp.exp2((score - new) * EXP_SCALE)
            denom[at] = denom[at] * keep + jnp.sum(weight, axis=1, keepdims=True)
            high[at] = new
            accum[at] = accum[at] * keep + dot(weight.astype(BF16), block[:latent], NT)

    def diagonal(score, start):
        row = start + lax.broadcasted_iota(jnp.int32, score.shape, 0)
        column = lax.broadcasted_iota(jnp.int32, score.shape, 1)
        return jnp.where(column <= row, score, masked_score)

    def pair_mask(step):
        def change(score, start):
            column = lax.broadcasted_iota(jnp.int32, score.shape, 1)
            first = jnp.where(z >= step, 0, tokens)
            last = jnp.where(z + step >= 8, 2 * tokens, tokens)
            return jnp.where((column >= first) & (column < last), score, masked_score)
        return change

    def own_pair(step):
        both = (z >= step) & (z + step >= 8)
        some = (z >= step) | (z + step >= 8)

        @pl.when(both)
        def _():
            tile(0, SLOT[step], 2)

        @pl.when(some & jnp.logical_not(both))
        def _():
            tile(0, SLOT[step], 2, pair_mask(step))

    def far_tile(slot, count):
        @pl.when(x_lo == 0)
        def _():
            tile(1, slot, count)

    members = {1: [1, 7], 2: [2, 6], 3: [3, 5], 4: [4]}

    def after_z(step, chunk):
        for way in (0, 1):
            if step < 4 or chunk == way:
                z_copy(way, step, chunk).wait_recv()
                if step < 3 or (step == 3 and chunk == way):
                    z_copy(way, step + 1, chunk).start()
                k = step if way == 0 else 8 - step
                y_copy(k, mine, chunk).start()
                s_copy(k, 0, mine, chunk).start()

    def after_y(step):
        for chunk in (0, 1):
            for k in members[step]:
                y_copy(k, other, chunk).wait_recv()
                s_copy(k, 1, other, chunk).start()

    def after_s(step):
        for chunk in (0, 1):
            for k in members[step]:
                s_copy(k, 0, sib_mine, chunk).wait_recv()
                s_copy(k, 1, sib_other, chunk).wait_recv()

    tile(0, 0, 1, diagonal)
    after_z(1, 0)
    after_z(1, 1)

    @pl.when(x_lo == 0)
    def _():
        q_copy.wait_recv()
        wv_copy.wait_recv()
        queries[1] = q_far[...].T

    after_z(2, 0)
    after_y(1)
    far_tile(0, 1)
    after_z(2, 1)
    after_s(1)
    own_pair(1)
    after_z(3, 0)
    after_y(2)
    far_tile(1, 2)
    after_z(3, 1)
    after_s(2)
    own_pair(2)
    after_z(4, 0)
    after_z(4, 1)
    after_y(3)
    far_tile(3, 2)
    after_s(3)
    after_y(4)
    own_pair(3)
    wo_far.wait_recv()
    wo_fwd.start()
    far_tile(5, 2)
    after_s(4)
    far_tile(7, 1)

    @pl.when(x_lo == 0)
    def _():
        latent_far = (accum[1] / denom[1]).astype(BF16)
        back[...] = dot(latent_far, wv_far[...]).astype(BF16)
        lse = high[1] * EXP_SCALE + jnp.log2(denom[1])
        back_lse[...] = jnp.broadcast_to(lse, (tokens, 128)).T[0:8]
        back_copy.start()
        lse_copy.start()

    @pl.when(z >= 4)
    def _():
        tile(0, 7, 1)

    head_out = dot((accum[0] / denom[0]).astype(BF16), wv_ref[...])

    @pl.when(x_lo == 0)
    def _():
        heads[...] = head_out.astype(BF16).reshape(heads.shape)

    @pl.when(x_lo == 1)
    def _():
        lse = high[0] * EXP_SCALE + jnp.log2(denom[0])
        back_copy.wait_recv()
        lse_copy.wait_recv()
        far = jnp.broadcast_to(far_lse[0:1], (128, tokens)).T
        top = jnp.maximum(lse, far)
        near_part, far_part = jnp.exp2(lse - top), jnp.exp2(far - top)
        merged = (head_out * near_part + far_out[...].astype(F32) * far_part) / (near_part + far_part)
        heads[...] = merged.astype(BF16).reshape(heads.shape)

    wo_sib.wait_recv()
    wo_fwd.wait_recv()
    wo_own.wait()
    for copy in (wo_sib, wo_far, wo_fwd):
        copy.wait_send()
    for step in range(1, 5):
        for way in (0, 1):
            for chunk in (0, 1):
                if step < 4 or chunk == way:
                    z_copy(way, step, chunk).wait_send()
    for k in range(1, 8):
        for chunk in (0, 1):
            y_copy(k, mine, chunk).wait_send()
            s_copy(k, 0, mine, chunk).wait_send()
            s_copy(k, 1, other, chunk).wait_send()

    @pl.when(x_lo == 1)
    def _():
        q_copy.wait_send()
        wv_copy.wait_send()

    @pl.when(x_lo == 0)
    def _():
        back_copy.wait_send()
        lse_copy.wait_send()


def routing_shares(ids_ref, scores_ref, experts):
    scores = scores_ref[...]
    combine = scores / jnp.sum(scores, axis=0, keepdims=True)
    lane = lax.broadcasted_iota(jnp.int32, (128, scores.shape[1]), 0)
    dense = jnp.zeros((128, scores.shape[1]), F32)
    for k in range(scores.shape[0]):
        chosen = ids_ref[k:k + 1]
        dense += jnp.where((lane == chosen) | (lane == chosen + experts), combine[k:k + 1], 0.0)
    coarse = dense.astype(BF16).astype(F32)
    return jnp.where(lane < experts, coarse, dense - coarse).T


def layer_part(
    loads, heads_ref, wo, resid_ref, gain_ref, ids_ref, scores_ref, out_ref,
    gate, up, down, pool, proj, proj_out, y_in, after, rows_in, part, hidden, sib_in, x_out, x_in,
    z_out, z_in,
    h_send, h_recv, y_send, y_recv, az_send, az_recv, ax_send, ax_recv, as_send, as_recv,
    bs_send, bs_recv, bx_send, bx_recv, bz_send, bz_recv,
):
    x, y, z, core = coords()
    x_lo, x_hi = x % 2, x // 2
    count, width = resid_ref.shape
    piece = count // 2
    sibling = device(x, y, z, 1 - core)
    z_way = (device(x, y, z + 1, core), device(x, y, z - 1, core))
    x_to = device(x - 1 + 2 * core, y, z, core)
    x_from = device(x + 1 - 2 * core, y, z, core)
    across = device(x + 2, y, z, core)
    across_sib = device(x + 2, y, z, 1 - core)
    y_at = [device(x, y + d, z, core) for d in (1, 2, 3)]

    mine = core * 2 + x_hi
    head_copies = [
        remote(heads_ref.at[c_to, :, x_to_hi], pool.at[mine], h_send.at[i], h_recv.at[i], target)
        for i, (c_to, x_to_hi, target) in enumerate((
            (1 - core, x_hi, sibling), (core, 1 - x_hi, across), (1 - core, 1 - x_hi, across_sib)))
    ]
    for copy in head_copies:
        copy.start()
    pool[mine] = heads_ref[core, :, x_hi]
    for copy in head_copies:
        copy.wait_recv()
    features = jnp.concatenate([pool[i].reshape(4 * count, pool.shape[3]) for i in range(4)], axis=1)
    attended = dot(features, wo[...].reshape(features.shape[1], width)).reshape(4, count, width)
    proj[...] = attended
    proj_out[...] = attended.astype(BF16)
    y_copies = [
        remote(proj_out.at[(y + d) % 4], y_in.at[d - 1], y_send.at[d - 1], y_recv.at[d - 1], y_at[d - 1])
        for d in (1, 2, 3)
    ]
    for copy in y_copies:
        copy.start()
    total = resid_ref[...].astype(F32) + proj[y]
    for d, copy in enumerate(y_copies):
        copy.wait_recv()
        total = total + y_in[d].astype(F32)
    after[...] = total.astype(BF16)
    widened = after[...].astype(F32)
    mean_square = jnp.mean(widened * widened, axis=1, keepdims=True)
    normed = (widened * lax.rsqrt(mean_square + norm_epsilon) * gain_ref[...]).astype(BF16)
    rows_in[0, core, 0, :, 0:width] = normed
    rows_in[0, core, 0, :, width:] = routing_shares(ids_ref, scores_ref, 16).astype(BF16)

    def gather_z(way, step, chunk):
        k_dst = step if way == 0 else 8 - step
        k_src = step - 1 if way == 0 else (9 - step) % 8
        at = pl.ds(chunk * piece, piece)
        return remote(
            rows_in.at[SLOT[k_src], core, 0, at], rows_in.at[SLOT[k_dst], core, 0, at],
            az_send.at[way, step - 1, chunk], az_recv.at[way, step - 1, chunk], z_way[way])

    def gather_x(k, chunk):
        at = pl.ds(chunk * piece, piece)
        return remote(
            rows_in.at[SLOT[k], core, 0, at], rows_in.at[SLOT[k], core, 1, at],
            ax_send.at[k, chunk], ax_recv.at[k, chunk], x_to)

    def gather_s(k, column, who, chunk):
        at = rows_in.at[SLOT[k], who, column, pl.ds(chunk * piece, piece)]
        return remote(at, at, as_send.at[column, k, chunk], as_recv.at[column, k, chunk], sibling)

    def return_s(slot, who):
        return remote(part.at[slot, who], sib_in.at[slot], bs_send.at[slot], bs_recv.at[slot], sibling)

    def return_x(slot):
        return remote(x_out.at[slot], x_in.at[slot], bx_send.at[slot], bx_recv.at[slot], x_from)

    def return_z(way, k, chunk):
        k_dst = k - 1 if way == 1 else (k + 1) % 8
        index = k_dst if way == 1 else (8 - k_dst) % 8
        return remote(
            z_out.at[way, index, chunk], z_in.at[way, index, chunk],
            bz_send.at[way, index, chunk], bz_recv.at[way, index, chunk], z_way[way])

    members = [[0], [1, 7], [2, 6], [3, 5], [4]]
    slots = [[SLOT[k] for k in ks] for ks in members]

    def hidden_units(step):
        first, number = slots[step][0], len(slots[step])
        block = rows_in[first:first + number].reshape(number * 4 * count, rows_in.shape[4])
        source, shares = block[:, :width], block[:, width:].astype(F32)
        lane = lax.broadcasted_iota(jnp.int32, shares.shape, 1)
        expert = lax.axis_index("ctx")
        share = jnp.sum(jnp.where((lane == expert) | (lane == expert + 16), shares, 0.0), axis=1, keepdims=True)
        gated = dot(source, gate[...], NT)
        value = gated / (1.0 + jnp.exp(-gated)) * dot(source, up[...], NT) * share
        hidden[0:number * 4 * count] = value.astype(BF16)

    def project_down(step):
        first, number = slots[step][0], len(slots[step])
        made = dot(hidden[0:number * 4 * count], down[...]).astype(BF16)
        part[first:first + number] = made.reshape(number, 2, 2, count, width)
        for slot in slots[step]:
            return_s(slot, 1 - core).start()

    def fold_siblings(step):
        for slot in slots[step]:
            return_s(slot, 1 - core).wait_recv()
            x_out[slot] = (part[slot, core, 1].astype(F32) + sib_in[slot, 1].astype(F32)).astype(BF16)
            return_x(slot).start()

    def after_z(step, chunk):
        for way in (0, 1):
            if step < 4 or chunk == way:
                gather_z(way, step, chunk).wait_recv()
                if step < 3 or (step == 3 and chunk == way):
                    gather_z(way, step + 1, chunk).start()
                k = step if way == 0 else 8 - step
                gather_x(k, chunk).start()
                gather_s(k, 0, core, chunk).start()

    def after_x(step):
        for chunk in (0, 1):
            for k in members[step]:
                gather_x(k, chunk).wait_recv()
                gather_s(k, 1, core, chunk).start()

    def after_s(step):
        for chunk in (0, 1):
            for k in members[step]:
                gather_s(k, 0, 1 - core, chunk).wait_recv()
                gather_s(k, 1, 1 - core, chunk).wait_recv()

    for chunk in (0, 1):
        for way in (0, 1):
            gather_z(way, 1, chunk).start()
        gather_x(0, chunk).start()
        gather_s(0, 0, core, chunk).start()
    for load in loads:
        load.wait()
    after_z(1, 0)
    after_z(1, 1)
    after_x(0)
    after_s(0)
    hidden_units(0)
    after_z(2, 0)
    project_down(0)
    after_z(2, 1)
    after_x(1)
    after_z(3, 0)
    after_s(1)
    fold_siblings(0)
    hidden_units(1)
    after_z(3, 1)
    project_down(1)
    after_z(4, 0)
    after_z(4, 1)
    after_x(2)
    after_s(2)
    hidden_units(2)
    after_x(3)
    fold_siblings(1)
    project_down(2)
    after_s(3)
    hidden_units(3)
    after_x(4)
    fold_siblings(2)
    project_down(3)
    after_s(4)
    hidden_units(4)
    fold_siblings(3)
    project_down(4)

    def local_sum(k, chunk):
        slot, at = SLOT[k], slice(chunk * piece, (chunk + 1) * piece)
        return part[slot, core, 0, at].astype(F32) + sib_in[slot, 0, at].astype(F32) + x_in[slot, at].astype(F32)

    def pass_on(way, k, chunk, incoming):
        value = local_sum(k, chunk)
        if incoming:
            index = k if way == 1 else 8 - k
            return_z(way, k + 1 if way == 1 else k - 1, chunk).wait_recv()
            value = value + z_in[way, index, chunk].astype(F32)
        copy = return_z(way, k, chunk)
        k_dst = k - 1 if way == 1 else (k + 1) % 8
        z_out[way, k_dst if way == 1 else (8 - k_dst) % 8, chunk] = value.astype(BF16)
        copy.start()

    def settle(step):
        for slot in slots[step]:
            return_x(slot).wait_recv()

    settle(3)
    pass_on(1, 3, 1, False)
    pass_on(0, 5, 0, False)
    fold_siblings(4)
    settle(4)
    pass_on(1, 4, 0, False)
    pass_on(0, 4, 1, False)
    pass_on(1, 3, 0, True)
    pass_on(0, 5, 1, True)
    settle(2)
    for chunk in (1, 0):
        pass_on(1, 2, chunk, True)
        pass_on(0, 6, 1 - chunk, True)
    settle(1)
    for chunk in (1, 0):
        pass_on(1, 1, chunk, True)
        pass_on(0, 7, 1 - chunk, True)
    settle(0)
    for chunk in (1, 0):
        return_z(1, 1, chunk).wait_recv()
        return_z(0, 7, chunk).wait_recv()
        at = slice(chunk * piece, (chunk + 1) * piece)
        combined = local_sum(0, chunk) + z_in[1, 0, chunk].astype(F32) + z_in[0, 0, chunk].astype(F32)
        out_ref[at] = (after[at].astype(F32) + routed_factor * combined).astype(BF16)

    for copy in head_copies + y_copies:
        copy.wait_send()
    for step in (1, 2, 3, 4):
        for way in (0, 1):
            for chunk in (0, 1):
                if step < 4 or chunk == way:
                    gather_z(way, step, chunk).wait_send()
                if step < 4 or chunk != way:
                    return_z(way, step if way == 1 else 8 - step, chunk).wait_send()
    for k in range(8):
        for chunk in (0, 1):
            gather_x(k, chunk).wait_send()
            gather_s(k, 0, core, chunk).wait_send()
            gather_s(k, 1, core, chunk).wait_send()
        return_s(k, 1 - core).wait_send()
        return_x(k).wait_send()


ATTENTION_SCRATCH = 22


def layer_kernel(
    q_ref, kv_ref, wv_ref, wo_ref, resid_ref, gain_ref, ids_ref, scores_ref, gate_ref, up_ref, down_ref, out_ref,
    heads, wo, gate, up, down, load_sem, *scratch,
):
    loads = [
        pltpu.make_async_copy(src, dst, load_sem.at[i])
        for i, (src, dst) in enumerate(((gate_ref, gate), (up_ref, up), (down_ref, down)))
    ]
    for load in loads:
        load.start()
    attention_part(q_ref, kv_ref, wv_ref, wo_ref, heads, wo, *scratch[:ATTENTION_SCRATCH])
    layer_part(
        loads, heads, wo, resid_ref, gain_ref, ids_ref, scores_ref, out_ref,
        gate, up, down, *scratch[ATTENTION_SCRATCH:])


def run_layer(queries, kv, w_value, w_out, resid, gain, ids, scores, gate, up, down):
    width, tokens = queries.shape
    latent, values = w_value.shape
    count, model = resid.shape
    units = gate.shape[0]
    dma = pltpu.SemaphoreType.DMA
    vmem = pl.BlockSpec(memory_space=pltpu.VMEM)
    hbm = pl.BlockSpec(memory_space=pl.ANY)
    attention_scratch = [
        pltpu.VMEM((8, 4, width, tokens // 4), BF16),
        pltpu.VMEM((width, tokens), BF16),
        pltpu.VMEM((2, tokens, width), BF16),
        pltpu.VMEM((latent, values), BF16),
        pltpu.VMEM((2, tokens, 1), F32),
        pltpu.VMEM((2, tokens, 1), F32),
        pltpu.VMEM((2, tokens, latent), F32),
        pltpu.VMEM((tokens, values), BF16),
        pltpu.VMEM((8, tokens), F32),
        pltpu.VMEM((tokens, values), BF16),
        pltpu.VMEM((8, tokens), F32),
        dma((2, 4, 2)), dma((2, 4, 2)), dma((7, 2)), dma((7, 2)), dma((2, 7, 2)), dma((2, 7, 2)),
        dma((4,)), dma((4,)), dma((3,)), dma((3,)), dma,
    ]
    layer_scratch = [
        pltpu.VMEM((4, 4, count, values), BF16),
        pltpu.VMEM((4, count, model), F32),
        pltpu.VMEM((4, count, model), BF16),
        pltpu.VMEM((3, count, model), BF16),
        pltpu.VMEM((count, model), BF16),
        pltpu.VMEM((8, 2, 2, count, model + 128), BF16),
        pltpu.VMEM((8, 2, 2, count, model), BF16),
        pltpu.VMEM((8 * count, units), BF16),
        pltpu.VMEM((8, 2, count, model), BF16),
        pltpu.VMEM((8, count, model), BF16),
        pltpu.VMEM((8, count, model), BF16),
        pltpu.VMEM((2, 4, 2, count // 2, model), BF16),
        pltpu.VMEM((2, 4, 2, count // 2, model), BF16),
        dma((3,)), dma((3,)), dma((3,)), dma((3,)),
        dma((2, 4, 2)), dma((2, 4, 2)), dma((8, 2)), dma((8, 2)), dma((2, 8, 2)), dma((2, 8, 2)),
        dma((8,)), dma((8,)), dma((8,)), dma((8,)), dma((2, 4, 2)), dma((2, 4, 2)),
    ]
    return pl.pallas_call(
        layer_kernel,
        out_shape=jax.ShapeDtypeStruct((count, model), BF16),
        in_specs=[vmem, vmem, vmem, hbm, vmem, vmem, vmem, vmem, hbm, hbm, hbm],
        out_specs=vmem,
        scratch_shapes=[
            pltpu.VMEM((2, 4, 2, count, values), BF16),
            pltpu.VMEM((4,) + w_out.shape, BF16),
            pltpu.VMEM((units, model), BF16),
            pltpu.VMEM((units, model), BF16),
            pltpu.VMEM((units, model), BF16),
            dma((3,)),
        ] + attention_scratch + layer_scratch,
        name="layer",
        compiler_params=pltpu.CompilerParams(collective_id=0, has_side_effects=True, vmem_limit_bytes=60 << 20),
    )(queries, kv, w_value, w_out, resid, gain.reshape(1, model), ids, scores, gate, up, down)


def per_device(
    q_latent,
    kv_latent,
    w_value,
    w_out,
    resid,
    norm_gain,
    w_gate,
    w_up,
    w_down_t,
    expert_ids,
    route_scores,
):
    return run_layer(
        q_latent.reshape(q_latent.shape[0], q_latent.shape[2]).T, kv_latent.T, w_value[0], w_out,
        resid, norm_gain, expert_ids.T, route_scores.T, w_gate[0].T, w_up[0].T, w_down_t[0].T,
    )


def solution(mesh):
    placed = (
        P("ctx", ("head", "ep"), None),
        P("ctx", None),
        P(("head", "ep"), None, None),
        P(("head", "ep"), None),
        P(("ctx", "head", "ep"), None),
        P(),
        P("ctx", None, "head"),
        P("ctx", None, "head"),
        P("ctx", None, "head"),
        P(("ctx", "head", "ep"), None),
        P(("ctx", "head", "ep"), None),
    )
    return jax.shard_map(
        per_device,
        mesh=mesh,
        in_specs=placed,
        out_specs=P(("ctx", "head", "ep"), None),
        check_vma=False,
    )
```

```python
import jax
import jax.numpy as jnp
from jax import lax
from jax.experimental import pallas as pl
from jax.experimental.pallas import tpu as pltpu
from jax.sharding import PartitionSpec as P

MESH = pl.DeviceIdType.MESH
BF16, F32 = jnp.bfloat16, jnp.float32
NT = (((1,), (1,)), ((), ()))
NN = (((1,), (0,)), ((), ()))
ROPE = 64
NOPE = 128
TOPK = 6
LOG2E = 1.4426950408889634
EXP_SCALE = (NOPE + ROPE) ** (-0.5) * LOG2E
routed_factor = 2.446
norm_epsilon = 1e-06
masked_score = -1e30


def dot(a, b, dims=NN):
    return lax.dot_general(a, b, dims, preferred_element_type=F32)


def coords():
    ctx, core, ep = lax.axis_index("ctx"), lax.axis_index("head"), lax.axis_index("ep")
    x_lo, z, y, x_hi = ctx // 8, ctx % 8, ep // 2, ep % 2
    return x_hi * 2 + x_lo, y, z, core


def device(x, y, z, core):
    x, y, z = (x + 4) % 4, (y + 4) % 4, (z + 8) % 8
    return ((x % 2) * 8 + z, core, y * 2 + x // 2)


def greet(partners):
    barrier = pltpu.get_barrier_semaphore()
    for partner in partners:
        pl.semaphore_signal(barrier, inc=1, device_id=partner, device_id_type=MESH)
    pl.semaphore_wait(barrier, len(partners))


def remote(src, dst, send_sem, recv_sem, target):
    return pltpu.make_async_remote_copy(
        src_ref=src, dst_ref=dst, send_sem=send_sem, recv_sem=recv_sem,
        device_id=target, device_id_type=MESH,
    )


SLOT = {0: 0, 1: 1, 7: 2, 2: 3, 6: 4, 3: 5, 5: 6, 4: 7}


def attention_part(
    loads, q_ref, kv_ref, wv_ref, wo_ref, heads, wo4_ref,
    keys, q_far, queries, wv_far, high, denom, accum, back, back_lse, far_out, far_lse,
    z_send, z_recv, y_send, y_recv, s_send, s_recv, q_send, q_recv, w_send, w_recv, own_sem,
):
    x, y, z, core = coords()
    x_lo, x_hi, parity = x % 2, x // 2, y % 2
    tokens, latent = q_ref.shape[1], wv_ref.shape[0]
    half, quarter, piece = tokens // 2, tokens // 4, q_ref.shape[0] // 2
    z_way = (device(x, y, z + 1, core), device(x, y, z - 1, core))
    y_up, y_down = device(x, y + 1, z, core), device(x, y - 1, z, core)
    x_up, x_down = device(x + 1, y, z, core), device(x - 1, y, z, core)
    sibling = device(x, y, z, 1 - core)
    y_to = device(x, y + 1 - 2 * core, z, core)
    x_to = device(x - 1 + 2 * core, y, z, core)
    x_from = device(x + 1 - 2 * core, y, z, core)
    x_other = device(x - 1 + 2 * x_lo, y, z, core)

    mine, other = parity * 2 + core, (1 - parity) * 2 + core
    sib_mine, sib_other = parity * 2 + 1 - core, (1 - parity) * 2 + 1 - core

    def z_copy(way, step, chunk):
        k_dst = step if way == 0 else 8 - step
        k_src = step - 1 if way == 0 else (9 - step) % 8
        at = pl.ds(chunk * piece, piece)
        return remote(
            keys.at[SLOT[k_src], mine, at], keys.at[SLOT[k_dst], mine, at],
            z_send.at[way, step - 1, chunk], z_recv.at[way, step - 1, chunk], z_way[way])

    def y_copy(k, which, chunk):
        at = keys.at[SLOT[k], which, pl.ds(chunk * piece, piece)]
        return remote(at, at, y_send.at[k - 1, chunk], y_recv.at[k - 1, chunk], y_to)

    def s_copy(k, row, which, chunk):
        at = keys.at[SLOT[k], which, pl.ds(chunk * piece, piece)]
        return remote(at, at, s_send.at[row, k - 1, chunk], s_recv.at[row, k - 1, chunk], sibling)

    q_copy = remote(q_ref, q_far, q_send.at[0], q_recv.at[0], x_to)
    wv_copy = remote(wv_ref, wv_far, q_send.at[1], q_recv.at[1], x_to)
    back_copy = remote(back, far_out, q_send.at[2], q_recv.at[2], x_from)
    lse_copy = remote(back_lse, far_lse, q_send.at[3], q_recv.at[3], x_from)
    place, partner = core * 2 + x_hi, core * 2 + 1 - x_hi
    wo_own = pltpu.make_async_copy(wo_ref, wo4_ref.at[place], own_sem)
    wo_sib = remote(wo_ref, wo4_ref.at[place], w_send.at[0], w_recv.at[0], sibling)
    wo_far = remote(wo_ref, wo4_ref.at[place], w_send.at[1], w_recv.at[1], x_other)
    wo_fwd = remote(wo4_ref.at[partner], wo4_ref.at[partner], w_send.at[2], w_recv.at[2], sibling)

    for j in range(4):
        keys[0, j] = kv_ref[:, j * quarter:(j + 1) * quarter]
    greet([*z_way, y_up, y_down, device(x, y + 2, z, core), x_up, x_down, sibling,
           device(x + 2, y, z, core), device(x + 2, y, z, 1 - core)])

    for chunk in (0, 1):
        for way in (0, 1):
            z_copy(way, 1, chunk).start()

    @pl.when(x_lo == 1)
    def _():
        q_copy.start()
        wv_copy.start()

    wo_own.start()
    wo_sib.start()
    wo_far.start()

    queries[0] = q_ref[...].T
    high[...] = jnp.full(high.shape, masked_score, F32)
    denom[...] = jnp.zeros(denom.shape, F32)
    accum[...] = jnp.zeros(accum.shape, F32)

    def tile(which, slot, count, change=None):
        block = jnp.concatenate([keys[slot + i, j] for i in range(count) for j in range(4)], axis=1)
        chunks = [slice(0, half), slice(half, tokens)]
        scores = [dot(queries[which, rows_at], block) for rows_at in chunks]
        for rows_at, score in zip(chunks, scores):
            if change is not None:
                score = change(score, rows_at.start)
            at = (which, rows_at, slice(None))
            old = high[at]
            new = jnp.maximum(old, jnp.max(score, axis=1, keepdims=True))
            keep = jnp.exp2((old - new) * EXP_SCALE)
            weight = jnp.exp2((score - new) * EXP_SCALE)
            denom[at] = denom[at] * keep + jnp.sum(weight, axis=1, keepdims=True)
            high[at] = new
            accum[at] = accum[at] * keep + dot(weight.astype(BF16), block[:latent], NT)

    def diagonal(score, start):
        row = start + lax.broadcasted_iota(jnp.int32, score.shape, 0)
        column = lax.broadcasted_iota(jnp.int32, score.shape, 1)
        return jnp.where(column <= row, score, masked_score)

    def pair_mask(step):
        def change(score, start):
            column = lax.broadcasted_iota(jnp.int32, score.shape, 1)
            first = jnp.where(z >= step, 0, tokens)
            last = jnp.where(z + step >= 8, 2 * tokens, tokens)
            return jnp.where((column >= first) & (column < last), score, masked_score)
        return change

    def own_pair(step):
        both = (z >= step) & (z + step >= 8)
        some = (z >= step) | (z + step >= 8)

        @pl.when(both)
        def _():
            tile(0, SLOT[step], 2)

        @pl.when(some & jnp.logical_not(both))
        def _():
            tile(0, SLOT[step], 2, pair_mask(step))

    def far_tile(slot, count):
        @pl.when(x_lo == 0)
        def _():
            tile(1, slot, count)

    members = {1: [1, 7], 2: [2, 6], 3: [3, 5], 4: [4]}

    def after_z(step, chunk):
        for way in (0, 1):
            if step < 4 or chunk == way:
                z_copy(way, step, chunk).wait_recv()
                if step < 3 or (step == 3 and chunk == way):
                    z_copy(way, step + 1, chunk).start()
                k = step if way == 0 else 8 - step
                y_copy(k, mine, chunk).start()
                s_copy(k, 0, mine, chunk).start()

    def after_y(step):
        for chunk in (0, 1):
            for k in members[step]:
                y_copy(k, other, chunk).wait_recv()
                s_copy(k, 1, other, chunk).start()

    def after_s(step):
        for chunk in (0, 1):
            for k in members[step]:
                s_copy(k, 0, sib_mine, chunk).wait_recv()
                s_copy(k, 1, sib_other, chunk).wait_recv()

    tile(0, 0, 1, diagonal)
    after_z(1, 0)
    after_z(1, 1)

    @pl.when(x_lo == 0)
    def _():
        q_copy.wait_recv()
        wv_copy.wait_recv()
        queries[1] = q_far[...].T

    after_z(2, 0)
    after_y(1)
    far_tile(0, 1)
    after_z(2, 1)
    after_s(1)
    own_pair(1)
    after_z(3, 0)
    after_y(2)
    for load in loads:
        load.start()
    far_tile(1, 2)
    after_z(3, 1)
    after_s(2)
    own_pair(2)
    after_z(4, 0)
    after_z(4, 1)
    after_y(3)
    wo_far.wait_recv()
    wo_fwd.start()
    far_tile(3, 2)
    after_s(3)
    after_y(4)
    own_pair(3)
    far_tile(5, 2)
    after_s(4)
    far_tile(7, 1)

    @pl.when(x_lo == 0)
    def _():
        latent_far = (accum[1] / denom[1]).astype(BF16)
        back[...] = dot(latent_far, wv_far[...]).astype(BF16)
        lse = high[1] * EXP_SCALE + jnp.log2(denom[1])
        back_lse[...] = jnp.broadcast_to(lse, (tokens, 128)).T[0:8]
        back_copy.start()
        lse_copy.start()

    @pl.when(z >= 4)
    def _():
        tile(0, 7, 1)

    head_out = dot((accum[0] / denom[0]).astype(BF16), wv_ref[...])

    @pl.when(x_lo == 0)
    def _():
        heads[...] = head_out.astype(BF16).reshape(heads.shape)

    @pl.when(x_lo == 1)
    def _():
        lse = high[0] * EXP_SCALE + jnp.log2(denom[0])
        back_copy.wait_recv()
        lse_copy.wait_recv()
        far = jnp.broadcast_to(far_lse[0:1], (128, tokens)).T
        top = jnp.maximum(lse, far)
        near_part, far_part = jnp.exp2(lse - top), jnp.exp2(far - top)
        merged = (head_out * near_part + far_out[...].astype(F32) * far_part) / (near_part + far_part)
        heads[...] = merged.astype(BF16).reshape(heads.shape)

    def finish_waits():
        for copy in (wo_sib, wo_far, wo_fwd):
            copy.wait_send()
        for step in range(1, 5):
            for way in (0, 1):
                for chunk in (0, 1):
                    if step < 4 or chunk == way:
                        z_copy(way, step, chunk).wait_send()
        for k in range(1, 8):
            for chunk in (0, 1):
                y_copy(k, mine, chunk).wait_send()
                s_copy(k, 0, mine, chunk).wait_send()
                s_copy(k, 1, other, chunk).wait_send()

        @pl.when(x_lo == 1)
        def _():
            q_copy.wait_send()
            wv_copy.wait_send()

        @pl.when(x_lo == 0)
        def _():
            back_copy.wait_send()
            lse_copy.wait_send()

    def w_out_ready():
        wo_sib.wait_recv()
        wo_fwd.wait_recv()
        wo_own.wait()

    return w_out_ready, finish_waits


def routing_shares(ids_ref, scores_ref, experts):
    scores = scores_ref[...]
    combine = scores / jnp.sum(scores, axis=0, keepdims=True)
    lane = lax.broadcasted_iota(jnp.int32, (128, scores.shape[1]), 0)
    dense = jnp.zeros((128, scores.shape[1]), F32)
    for k in range(scores.shape[0]):
        chosen = ids_ref[k:k + 1]
        dense += jnp.where((lane == chosen) | (lane == chosen + experts), combine[k:k + 1], 0.0)
    coarse = dense.astype(BF16).astype(F32)
    return jnp.where(lane < experts, coarse, dense - coarse).T


def layer_part(
    loads, w_out_ready, heads_ref, wo, resid_ref, gain_ref, ids_ref, scores_ref, out_ref,
    gate, up, down, pool, proj, proj_out, y_in, after, rows_in, part, hidden, sib_in, x_out, x_in,
    z_out, z_in,
    h_send, h_recv, y_send, y_recv, az_send, az_recv, ax_send, ax_recv, as_send, as_recv,
    bs_send, bs_recv, bx_send, bx_recv, bz_send, bz_recv,
):
    x, y, z, core = coords()
    x_lo, x_hi = x % 2, x // 2
    count, width = resid_ref.shape
    piece = count // 2
    sibling = device(x, y, z, 1 - core)
    z_way = (device(x, y, z + 1, core), device(x, y, z - 1, core))
    x_to = device(x - 1 + 2 * core, y, z, core)
    x_from = device(x + 1 - 2 * core, y, z, core)
    across = device(x + 2, y, z, core)
    across_sib = device(x + 2, y, z, 1 - core)
    y_at = [device(x, y + d, z, core) for d in (1, 2, 3)]

    mine = core * 2 + x_hi
    head_copies = [
        remote(heads_ref.at[c_to, :, x_to_hi], pool.at[mine], h_send.at[i], h_recv.at[i], target)
        for i, (c_to, x_to_hi, target) in enumerate((
            (1 - core, x_hi, sibling), (core, 1 - x_hi, across), (1 - core, 1 - x_hi, across_sib)))
    ]
    for copy in head_copies:
        copy.start()
    pool[mine] = heads_ref[core, :, x_hi]
    for copy in head_copies:
        copy.wait_recv()
    w_out_ready()
    features = jnp.concatenate([pool[i].reshape(4 * count, pool.shape[3]) for i in range(4)], axis=1)
    attended = dot(features, wo[...].reshape(features.shape[1], width)).reshape(4, count, width)
    proj[...] = attended
    proj_out[...] = attended.astype(BF16)
    y_copies = [
        remote(proj_out.at[(y + d) % 4], y_in.at[d - 1], y_send.at[d - 1], y_recv.at[d - 1], y_at[d - 1])
        for d in (1, 2, 3)
    ]
    for copy in y_copies:
        copy.start()
    total = resid_ref[...].astype(F32) + proj[y]
    for d, copy in enumerate(y_copies):
        copy.wait_recv()
        total = total + y_in[d].astype(F32)
    after[...] = total.astype(BF16)
    widened = after[...].astype(F32)
    mean_square = jnp.mean(widened * widened, axis=1, keepdims=True)
    normed = (widened * lax.rsqrt(mean_square + norm_epsilon) * gain_ref[...]).astype(BF16)
    rows_in[0, core, 0, :, 0:width] = normed
    rows_in[0, core, 0, :, width:] = routing_shares(ids_ref, scores_ref, 16).astype(BF16)

    def gather_z(way, step, chunk):
        k_dst = step if way == 0 else 8 - step
        k_src = step - 1 if way == 0 else (9 - step) % 8
        at = pl.ds(chunk * piece, piece)
        return remote(
            rows_in.at[SLOT[k_src], core, 0, at], rows_in.at[SLOT[k_dst], core, 0, at],
            az_send.at[way, step - 1, chunk], az_recv.at[way, step - 1, chunk], z_way[way])

    def gather_x(k, chunk):
        at = pl.ds(chunk * piece, piece)
        return remote(
            rows_in.at[SLOT[k], core, 0, at], rows_in.at[SLOT[k], core, 1, at],
            ax_send.at[k, chunk], ax_recv.at[k, chunk], x_to)

    def gather_s(k, column, who, chunk):
        at = rows_in.at[SLOT[k], who, column, pl.ds(chunk * piece, piece)]
        return remote(at, at, as_send.at[column, k, chunk], as_recv.at[column, k, chunk], sibling)

    def return_s(slot, who):
        return remote(part.at[slot, who], sib_in.at[slot], bs_send.at[slot], bs_recv.at[slot], sibling)

    def return_x(slot):
        return remote(x_out.at[slot], x_in.at[slot], bx_send.at[slot], bx_recv.at[slot], x_from)

    def return_z(way, k, chunk):
        k_dst = k - 1 if way == 1 else (k + 1) % 8
        index = k_dst if way == 1 else (8 - k_dst) % 8
        return remote(
            z_out.at[way, index, chunk], z_in.at[way, index, chunk],
            bz_send.at[way, index, chunk], bz_recv.at[way, index, chunk], z_way[way])

    members = [[0], [1, 7], [2, 6], [3, 5], [4]]
    slots = [[SLOT[k] for k in ks] for ks in members]

    def hidden_units(step):
        first, number = slots[step][0], len(slots[step])
        block = rows_in[first:first + number].reshape(number * 4 * count, rows_in.shape[4])
        source, shares = block[:, :width], block[:, width:].astype(F32)
        lane = lax.broadcasted_iota(jnp.int32, shares.shape, 1)
        expert = lax.axis_index("ctx")
        share = jnp.sum(jnp.where((lane == expert) | (lane == expert + 16), shares, 0.0), axis=1, keepdims=True)
        gated = dot(source, gate[...], NT)
        value = gated / (1.0 + jnp.exp(-gated)) * dot(source, up[...], NT) * share
        hidden[0:number * 4 * count] = value.astype(BF16)

    def project_down(step):
        first, number = slots[step][0], len(slots[step])
        made = dot(hidden[0:number * 4 * count], down[...]).astype(BF16)
        part[first:first + number] = made.reshape(number, 2, 2, count, width)
        for slot in slots[step]:
            return_s(slot, 1 - core).start()

    def fold_siblings(step):
        for slot in slots[step]:
            return_s(slot, 1 - core).wait_recv()
            x_out[slot] = (part[slot, core, 1].astype(F32) + sib_in[slot, 1].astype(F32)).astype(BF16)
            return_x(slot).start()

    def after_z(step, chunk):
        for way in (0, 1):
            if step < 4 or chunk == way:
                gather_z(way, step, chunk).wait_recv()
                if step < 3 or (step == 3 and chunk == way):
                    gather_z(way, step + 1, chunk).start()
                k = step if way == 0 else 8 - step
                gather_x(k, chunk).start()
                gather_s(k, 0, core, chunk).start()

    def after_x(step):
        for chunk in (0, 1):
            for k in members[step]:
                gather_x(k, chunk).wait_recv()
                gather_s(k, 1, core, chunk).start()

    def after_s(step):
        for chunk in (0, 1):
            for k in members[step]:
                gather_s(k, 0, 1 - core, chunk).wait_recv()
                gather_s(k, 1, 1 - core, chunk).wait_recv()

    for chunk in (0, 1):
        for way in (0, 1):
            gather_z(way, 1, chunk).start()
        gather_x(0, chunk).start()
        gather_s(0, 0, core, chunk).start()
    for load in loads:
        load.wait()
    after_z(1, 0)
    after_z(1, 1)
    after_x(0)
    after_s(0)
    hidden_units(0)
    after_z(2, 0)
    project_down(0)
    after_z(2, 1)
    after_x(1)
    after_z(3, 0)
    after_s(1)
    hidden_units(1)
    after_z(3, 1)
    project_down(1)
    after_z(4, 0)
    after_z(4, 1)
    after_x(2)
    after_s(2)
    hidden_units(2)
    after_x(3)
    project_down(2)
    after_s(3)
    hidden_units(3)
    after_x(4)
    project_down(3)
    after_s(4)
    hidden_units(4)
    fold_siblings(3)
    project_down(4)

    def local_sum(k, chunk):
        slot, at = SLOT[k], slice(chunk * piece, (chunk + 1) * piece)
        return part[slot, core, 0, at].astype(F32) + sib_in[slot, 0, at].astype(F32) + x_in[slot, at].astype(F32)

    def pass_on(way, k, chunk, incoming):
        value = local_sum(k, chunk)
        if incoming:
            index = k if way == 1 else 8 - k
            return_z(way, k + 1 if way == 1 else k - 1, chunk).wait_recv()
            value = value + z_in[way, index, chunk].astype(F32)
        copy = return_z(way, k, chunk)
        k_dst = k - 1 if way == 1 else (k + 1) % 8
        z_out[way, k_dst if way == 1 else (8 - k_dst) % 8, chunk] = value.astype(BF16)
        copy.start()

    def settle(step):
        for slot in slots[step]:
            return_x(slot).wait_recv()

    settle(3)
    pass_on(1, 3, 1, False)
    pass_on(0, 5, 0, False)
    fold_siblings(4)
    for step in (2, 1, 0):
        fold_siblings(step)
    settle(4)
    pass_on(1, 4, 0, False)
    pass_on(0, 4, 1, False)
    pass_on(1, 3, 0, True)
    pass_on(0, 5, 1, True)
    settle(2)
    for chunk in (1, 0):
        pass_on(1, 2, chunk, True)
        pass_on(0, 6, 1 - chunk, True)
    settle(1)
    for chunk in (1, 0):
        pass_on(1, 1, chunk, True)
        pass_on(0, 7, 1 - chunk, True)
    settle(0)
    for chunk in (1, 0):
        return_z(1, 1, chunk).wait_recv()
        return_z(0, 7, chunk).wait_recv()
        at = slice(chunk * piece, (chunk + 1) * piece)
        combined = local_sum(0, chunk) + z_in[1, 0, chunk].astype(F32) + z_in[0, 0, chunk].astype(F32)
        out_ref[at] = (after[at].astype(F32) + routed_factor * combined).astype(BF16)

    for copy in head_copies + y_copies:
        copy.wait_send()
    for step in (1, 2, 3, 4):
        for way in (0, 1):
            for chunk in (0, 1):
                if step < 4 or chunk == way:
                    gather_z(way, step, chunk).wait_send()
                if step < 4 or chunk != way:
                    return_z(way, step if way == 1 else 8 - step, chunk).wait_send()
    for k in range(8):
        for chunk in (0, 1):
            gather_x(k, chunk).wait_send()
            gather_s(k, 0, core, chunk).wait_send()
            gather_s(k, 1, core, chunk).wait_send()
        return_s(k, 1 - core).wait_send()
        return_x(k).wait_send()


ATTENTION_SCRATCH = 22


def layer_kernel(
    q_ref, kv_ref, wv_ref, wo_ref, resid_ref, gain_ref, ids_ref, scores_ref, gate_ref, up_ref, down_ref, out_ref,
    heads, wo, gate, up, down, load_sem, *scratch,
):
    loads = [
        pltpu.make_async_copy(src, dst, load_sem.at[i])
        for i, (src, dst) in enumerate(((gate_ref, gate), (up_ref, up), (down_ref, down)))
    ]
    w_out_ready, finish_waits = attention_part(loads, q_ref, kv_ref, wv_ref, wo_ref, heads, wo, *scratch[:ATTENTION_SCRATCH])
    layer_part(
        loads, w_out_ready, heads, wo, resid_ref, gain_ref, ids_ref, scores_ref, out_ref,
        gate, up, down, *scratch[ATTENTION_SCRATCH:])
    finish_waits()


def run_layer(queries, kv, w_value, w_out, resid, gain, ids, scores, gate, up, down):
    width, tokens = queries.shape
    latent, values = w_value.shape
    count, model = resid.shape
    units = gate.shape[0]
    dma = pltpu.SemaphoreType.DMA
    vmem = pl.BlockSpec(memory_space=pltpu.VMEM)
    hbm = pl.BlockSpec(memory_space=pl.ANY)
    attention_scratch = [
        pltpu.VMEM((8, 4, width, tokens // 4), BF16),
        pltpu.VMEM((width, tokens), BF16),
        pltpu.VMEM((2, tokens, width), BF16),
        pltpu.VMEM((latent, values), BF16),
        pltpu.VMEM((2, tokens, 1), F32),
        pltpu.VMEM((2, tokens, 1), F32),
        pltpu.VMEM((2, tokens, latent), F32),
        pltpu.VMEM((tokens, values), BF16),
        pltpu.VMEM((8, tokens), F32),
        pltpu.VMEM((tokens, values), BF16),
        pltpu.VMEM((8, tokens), F32),
        dma((2, 4, 2)), dma((2, 4, 2)), dma((7, 2)), dma((7, 2)), dma((2, 7, 2)), dma((2, 7, 2)),
        dma((4,)), dma((4,)), dma((3,)), dma((3,)), dma,
    ]
    layer_scratch = [
        pltpu.VMEM((4, 4, count, values), BF16),
        pltpu.VMEM((4, count, model), F32),
        pltpu.VMEM((4, count, model), BF16),
        pltpu.VMEM((3, count, model), BF16),
        pltpu.VMEM((count, model), BF16),
        pltpu.VMEM((8, 2, 2, count, model + 128), BF16),
        pltpu.VMEM((8, 2, 2, count, model), BF16),
        pltpu.VMEM((8 * count, units), BF16),
        pltpu.VMEM((8, 2, count, model), BF16),
        pltpu.VMEM((8, count, model), BF16),
        pltpu.VMEM((8, count, model), BF16),
        pltpu.VMEM((2, 4, 2, count // 2, model), BF16),
        pltpu.VMEM((2, 4, 2, count // 2, model), BF16),
        dma((3,)), dma((3,)), dma((3,)), dma((3,)),
        dma((2, 4, 2)), dma((2, 4, 2)), dma((8, 2)), dma((8, 2)), dma((2, 8, 2)), dma((2, 8, 2)),
        dma((8,)), dma((8,)), dma((8,)), dma((8,)), dma((2, 4, 2)), dma((2, 4, 2)),
    ]
    return pl.pallas_call(
        layer_kernel,
        out_shape=jax.ShapeDtypeStruct((count, model), BF16),
        in_specs=[vmem, vmem, vmem, hbm, vmem, vmem, vmem, vmem, hbm, hbm, hbm],
        out_specs=vmem,
        scratch_shapes=[
            pltpu.VMEM((2, 4, 2, count, values), BF16),
            pltpu.VMEM((4,) + w_out.shape, BF16),
            pltpu.VMEM((units, model), BF16),
            pltpu.VMEM((units, model), BF16),
            pltpu.VMEM((units, model), BF16),
            dma((3,)),
        ] + attention_scratch + layer_scratch,
        name="layer",
        compiler_params=pltpu.CompilerParams(collective_id=0, has_side_effects=True, vmem_limit_bytes=60 << 20),
    )(queries, kv, w_value, w_out, resid, gain.reshape(1, model), ids, scores, gate, up, down)


def per_device(
    q_latent,
    kv_latent,
    w_value,
    w_out,
    resid,
    norm_gain,
    w_gate,
    w_up,
    w_down_t,
    expert_ids,
    route_scores,
):
    return run_layer(
        q_latent.reshape(q_latent.shape[0], q_latent.shape[2]).T, kv_latent.T, w_value[0], w_out,
        resid, norm_gain, expert_ids.T, route_scores.T, w_gate[0].T, w_up[0].T, w_down_t[0].T,
    )


def solution(mesh):
    placed = (
        P("ctx", ("head", "ep"), None),
        P("ctx", None),
        P(("head", "ep"), None, None),
        P(("head", "ep"), None),
        P(("ctx", "head", "ep"), None),
        P(),
        P("ctx", None, "head"),
        P("ctx", None, "head"),
        P("ctx", None, "head"),
        P(("ctx", "head", "ep"), None),
        P(("ctx", "head", "ep"), None),
    )
    return jax.shard_map(
        per_device,
        mesh=mesh,
        in_specs=placed,
        out_specs=P(("ctx", "head", "ep"), None),
        check_vma=False,
    )
```
